512 devices in a mesh: ctx: 128 (over x_lo, z, y), head: 4 (over x_hi, core).
Axes of the slice: x: 4 (x_hi: 2, x_lo: 2; x = x_hi * 2 + x_lo), y: 4, z: 16, core: 2. Of those that a mesh axis runs over, the one named last changes fastest.
Arguments:
- queries: bfloat16 [49152, 2048], P('ctx', 'head'), may hold values from -10 to 10, as said below
- key_rows: bfloat16 [49152, 2048], P('ctx', 'head'), may hold values from -10 to 10, as said below
- value_rows: bfloat16 [49152, 2048], P('ctx', 'head'), may hold values from -6 to 6
- out_weight: bfloat16 [2048, 2048], P('head'), may hold values from -0.125 to 0.125
- cotangent: bfloat16 [49152, 2048], P('ctx', 'head'), may hold values from -6 to 6
- offsets: int32 [2056], replicated, may hold values from 0 to 394560, as said below
Outputs:
- mixed: bfloat16 [49152, 2048], P('ctx', 'head')
- grad_queries: bfloat16 [49152, 2048], P('ctx', 'head')
- grad_keys: bfloat16 [49152, 2048], P('ctx', 'head')
- grad_values: bfloat16 [49152, 2048], P('ctx', 'head')
The draws below stay inside these ranges and needn't reach their ends.
Inputs may be any that keep to these rules, and one draw needn't show every extreme that they name: offsets start at 0 and increase; consecutive entries differ by 1 to 192 except before the last entry, which is (2055) * 192 and lies beyond the history, as does the entry before it. `queries`: real values. `key_rows`: real values.
All inputs are finite; a program needn't handle non-finite values.
Results may differ from the reference program's by a relative error of at most 0.018.
Values may be sent and summed in bfloat16 or wider, within the bound.
A program may use at most 64 MiB of HBM per device.

```python
import math
import jax
import jax.numpy as jnp
from jax import lax

D = 2048
HEADS = 16
HD = 128
T_DEV = 384
REACH = 2
PREV = 3
EP_MAX = 192
TOKENS = 49152
EPISODES = 2056


def attention_pair(key):
    columns = HEADS * HD
    key_q = jax.random.fold_in(key, 201)
    key_k = jax.random.fold_in(key, 202)
    query_draw = jnp.clip(jax.random.normal(key_q, (TOKENS, columns), jnp.float32), -4.0, 4.0)
    key_draw = jnp.clip(jax.random.normal(key_k, (TOKENS, columns), jnp.float32), -4.0, 4.0)
    return (query_draw, key_draw)


def draw_queries(key, part):
    return attention_pair(key)[0].astype(jnp.bfloat16)


def draw_key_rows(key, part):
    return attention_pair(key)[1].astype(jnp.bfloat16)


def draw_offsets(key, part):
    key_groups = jax.random.fold_in(key, 101)
    key_trim = jax.random.fold_in(key, 102)
    key_place = jax.random.fold_in(key, 103)
    group_count = EPISODES // 16 + 1
    regime = jax.random.randint(key_groups, (group_count,), 0, 3)
    regime = jnp.repeat(regime, 16)[:EPISODES]
    longest = jnp.right_shift(jnp.full((EPISODES,), EP_MAX, jnp.int32), regime.astype(jnp.int32))
    trimmed = jax.random.randint(key_trim, (EPISODES,), 0, longest // 2 + 1)
    lengths = (longest - trimmed).astype(jnp.int32)
    first_run = jax.random.randint(key_place, (), 3, max(4, TOKENS // (4 * T_DEV)))
    order = jnp.arange(EPISODES)
    lengths = jnp.where((order >= first_run) & (order <= first_run + PREV), EP_MAX, lengths)
    before_fill = jnp.sum(jnp.where(order < first_run - 3, lengths, 0))
    target = before_fill + 3 + jnp.remainder(T_DEV - 4 - before_fill, T_DEV)
    filler = target - before_fill
    lengths = jnp.where(order == first_run - 3, filler // 3, lengths)
    lengths = jnp.where(order == first_run - 2, (filler + 1) // 3, lengths)
    lengths = jnp.where(order == first_run - 1, (filler + 2) // 3, lengths)
    starts = jnp.cumsum(lengths)[:-1]
    listed = jnp.concatenate([jnp.zeros((1,), jnp.int32), starts.astype(jnp.int32)]).astype(jnp.int32)
    last_entry = jnp.full((EPISODES,), (EPISODES - 1) * EP_MAX, jnp.int32)
    return jnp.where(order == EPISODES - 1, last_entry, listed).astype(jnp.int32)


def level_of(key, dims, shards, least, top_value):
    def one(position, blocks):
        steps = jax.random.uniform(jax.random.fold_in(jax.random.fold_in(key, 6), position), (blocks,), jnp.float32, least / len(shards), top_value / len(shards))
        return jnp.repeat(jnp.exp(steps), dims[position] // blocks).reshape((-1,) + (1,) * (len(dims) - position - 1))

    level = one(*shards[0])
    for cut in shards[1:]:
        level = level * one(*cut)
    return level


def centred(rng, extent, scale, reach, cuts=(), kind=jnp.bfloat16):
    array = jax.random.normal(rng, extent, jnp.float32) * scale
    if len(cuts) > 0:
        array = level_of(rng, extent, cuts, -0.22, 0.18) * array
    return jnp.clip(array, min=-reach, max=reach).astype(kind)


def setup_inputs(seed: int = 0) -> dict:
    key_list = jax.random.split(jax.random.key(seed), 7)
    queries = draw_queries(jax.random.fold_in(key_list[6], 71), 0)
    key_rows = draw_key_rows(jax.random.fold_in(key_list[6], 71), 0)
    value_rows = centred(key_list[2], (TOKENS, HEADS * HD), 1.0, 6.0, ((0, 128), (1, 4)))
    out_weight = centred(key_list[3], (HEADS * HD, D), (HEADS * HD) ** -0.5, 0.125, ((0, 4),))
    cotangent = centred(key_list[4], (TOKENS, D), 1.0, 6.0, ((0, 128), (1, 4)))
    offsets = draw_offsets(jax.random.fold_in(key_list[6], 71), 0)
    return dict(queries=queries, key_rows=key_rows, value_rows=value_rows, out_weight=out_weight, cotangent=cotangent, offsets=offsets)


NEG_FILL = -1e+30

def episode_ids(positions, offsets):
    hit_count = lax.optimization_barrier(jnp.sum((offsets[None, :] <= positions[:, None]).astype(jnp.int32), axis=1))
    return (hit_count - 1).astype(jnp.int32)

def rounded(values):
    return lax.optimization_barrier(values.astype(jnp.bfloat16)).astype(jnp.float32)

def reference(queries, key_rows, value_rows, out_weight, cotangent, offsets):
    head_cols = HEADS * HD
    key_span = (REACH + 1) * T_DEV
    pad_rows = REACH * T_DEV
    score_scale = 1.0 / math.sqrt(HD)
    keys_padded = jnp.concatenate([jnp.zeros((pad_rows, head_cols), key_rows.dtype), key_rows], axis=0)
    values_padded = jnp.concatenate([jnp.zeros((pad_rows, head_cols), value_rows.dtype), value_rows], axis=0)

    def scan_step(grad_carry, block_index):
        grad_keys, grad_values = grad_carry
        start_row = (block_index * T_DEV).astype(jnp.int32)
        query_block = lax.dynamic_slice_in_dim(queries, start_row, T_DEV, 0)
        grad_block = lax.dynamic_slice_in_dim(cotangent, start_row, T_DEV, 0)
        key_block = lax.dynamic_slice_in_dim(keys_padded, start_row, key_span, 0)
        value_block = lax.dynamic_slice_in_dim(values_padded, start_row, key_span, 0)
        query_pos = start_row + jnp.arange(T_DEV, dtype=jnp.int32)
        key_pos = start_row - pad_rows + jnp.arange(key_span, dtype=jnp.int32)
        query_ep = episode_ids(query_pos, offsets)
        key_ep = episode_ids(key_pos, offsets)
        allowed = (key_pos[None, :] <= query_pos[:, None]) & (key_pos[None, :] >= 0) & (query_ep[:, None] - key_ep[None, :] <= PREV)
        query_heads = query_block.astype(jnp.float32).reshape(T_DEV, HEADS, HD)
        key_heads = key_block.astype(jnp.float32).reshape(key_span, HEADS, HD)
        value_heads = value_block.astype(jnp.float32).reshape(key_span, HEADS, HD)
        scores = jnp.einsum('qhd,khd->hqk', query_heads, key_heads) * score_scale
        scores = jnp.where(allowed[None], scores, NEG_FILL)
        row_max = lax.optimization_barrier(jnp.max(scores, axis=2, keepdims=True))
        row_total = lax.optimization_barrier(jnp.sum(jnp.exp(scores - row_max), axis=2, keepdims=True))
        log_total = row_max + jnp.log(row_total)
        attn_probs = jnp.where(allowed[None], jnp.exp(scores - log_total), 0.0)
        probs_b = rounded(attn_probs)
        attended = jnp.einsum('hqk,khd->qhd', probs_b, value_heads).reshape(T_DEV, head_cols)
        attended_b = attended.astype(jnp.bfloat16)
        mixed_block = jnp.dot(attended_b, out_weight, preferred_element_type=jnp.float32).astype(jnp.bfloat16)
        grad_out = jnp.dot(grad_block, out_weight.T, preferred_element_type=jnp.float32).astype(jnp.bfloat16)
        grad_heads = grad_out.astype(jnp.float32).reshape(T_DEV, HEADS, HD)
        attended_heads = attended_b.astype(jnp.float32).reshape(T_DEV, HEADS, HD)
        row_delta = jnp.einsum('qhd,qhd->hq', grad_heads, attended_heads)[:, :, None]
        grad_probs = jnp.einsum('qhd,khd->hqk', grad_heads, value_heads)
        grad_scores = rounded(score_scale * attn_probs * (grad_probs - row_delta))
        grad_query = jnp.einsum('hqk,khd->qhd', grad_scores, key_heads).reshape(T_DEV, head_cols).astype(jnp.bfloat16)
        part_keys = jnp.einsum('hqk,qhd->khd', grad_scores, query_heads).reshape(key_span, head_cols)
        part_values = jnp.einsum('hqk,qhd->khd', probs_b, grad_heads).reshape(key_span, head_cols)
        old_keys = lax.dynamic_slice_in_dim(grad_keys, start_row, key_span, 0)
        grad_keys = lax.dynamic_update_slice_in_dim(grad_keys, old_keys + part_keys, start_row, 0)
        old_values = lax.dynamic_slice_in_dim(grad_values, start_row, key_span, 0)
        grad_values = lax.dynamic_update_slice_in_dim(grad_values, old_values + part_values, start_row, 0)
        return ((grad_keys, grad_values), (mixed_block, grad_query))
    blocks = TOKENS // T_DEV
    start_carry = (jnp.zeros((TOKENS + pad_rows, head_cols), jnp.float32), jnp.zeros((TOKENS + pad_rows, head_cols), jnp.float32))
    final_carry, outputs = lax.scan(scan_step, start_carry, jnp.arange(blocks, dtype=jnp.int32))
    mixed = outputs[0].reshape(TOKENS, D)
    grad_queries = outputs[1].reshape(TOKENS, head_cols)
    grad_keys = final_carry[0][pad_rows:].astype(jnp.bfloat16)
    grad_values = final_carry[1][pad_rows:].astype(jnp.bfloat16)
    return (mixed, grad_queries, grad_keys, grad_values)
```

```python
import functools
import math

import jax
import jax.numpy as jnp
from jax import lax
from jax.experimental import pallas as pl
from jax.experimental.pallas import tpu as pltpu
from jax.sharding import PartitionSpec as P

HD = 128
PREV = 3
NEG_FILL = -1e30
LOG2E = math.log2(math.e)
F32 = jnp.float32
BF16 = jnp.bfloat16
MESH = pl.DeviceIdType.MESH


def dot_nn(a, b):
    return lax.dot_general(a, b, (((1,), (0,)), ((), ())), preferred_element_type=F32)


def dot_nt(a, b):
    return lax.dot_general(a, b, (((1,), (1,)), ((), ())), preferred_element_type=F32)


def dot_tn(a, b):
    return lax.dot_general(a, b, (((0,), (0,)), ((), ())), preferred_element_type=F32)


def kernel(
    n_ctx, q_hbm, k_hbm, v_hbm, w_hbm, c_hbm, offs,
    mixed_hbm, dq_hbm, dk_hbm, dv_hbm,
    own_q, own_k, own_v, own_do, w_ref, cot, kv, qo, stats, stats_in,
    att, acc, mix_out, mix_in, out_v,
    load_sem, cot_send, cot_recv, kv_send, kv_recv, qo_send, qo_recv,
    st_send, st_recv, mix_send, mix_recv, out_sem,
):
    rows = q_hbm.shape[0]
    feats = q_hbm.shape[1]
    heads = feats // HD
    scale = 1.0 / math.sqrt(HD)
    scale2 = scale * LOG2E
    me = lax.axis_index("ctx")
    grp = lax.axis_index("head")
    right = lax.rem(me + 1, n_ctx)
    left = lax.rem(me + n_ctx - 1, n_ctx)
    left2 = lax.rem(me + n_ctx - 2, n_ctx)
    right2 = lax.rem(me + 2, n_ctx)
    core = lax.rem(grp, 2)
    pair = grp // 2
    core_mate = pair * 2 + (1 - core)
    x_mate = (1 - pair) * 2 + core
    x_core_mate = (1 - pair) * 2 + (1 - core)

    barrier = pltpu.get_barrier_semaphore()
    for target in ((right, grp), (left, grp), (right2, grp), (me, core_mate), (me, x_mate)):
        pl.semaphore_signal(barrier, inc=1, device_id=target, device_id_type=MESH)

    def cols(ref, h):
        return ref.at[:, h * HD : (h + 1) * HD]

    loads = []
    for slot, (src, dst) in enumerate(((c_hbm, cot.at[0]), (w_hbm, w_ref))):
        loads.append(pltpu.make_async_copy(src, dst, load_sem.at[slot]))
    head_loads = []
    for a, (src, dst) in enumerate(((q_hbm, own_q), (k_hbm, own_k), (v_hbm, own_v))):
        for h in range(heads):
            head_loads.append(
                pltpu.make_async_copy(cols(src, h), dst.at[h], load_sem.at[2 + a * heads + h])
            )
    for copy in loads + head_loads:
        copy.start()

    def remote(src, dst, send, recv, target):
        return pltpu.make_async_remote_copy(
            src_ref=src, dst_ref=dst, send_sem=send, recv_sem=recv,
            device_id=target, device_id_type=MESH,
        )

    def kv_copy(hop, a, h):
        src = cols((k_hbm, v_hbm)[a], h) if hop == 0 else kv.at[0, a, h]
        return remote(
            src, kv.at[hop, a, h], kv_send.at[hop, a, h], kv_recv.at[hop, a, h], (right, grp)
        )

    def qo_copy(hop, a, h):
        if hop == 0:
            src = cols(q_hbm, h) if a == 0 else own_do.at[h]
        else:
            src = qo.at[0, a, h]
        return remote(
            src, qo.at[hop, a, h], qo_send.at[hop, a, h], qo_recv.at[hop, a, h], (left, grp)
        )

    cot_core = remote(c_hbm, cot.at[1], cot_send.at[0], cot_recv.at[0], (me, core_mate))
    cot_x = remote(c_hbm, cot.at[2], cot_send.at[1], cot_recv.at[1], (me, x_mate))
    cot_relay = remote(cot.at[2], cot.at[3], cot_send.at[2], cot_recv.at[2], (me, core_mate))

    pl.semaphore_wait(barrier, 5)
    cot_x.start()
    cot_core.start()
    for h in range(2):
        kv_copy(0, 0, h).start()
        kv_copy(0, 1, h).start()
    for h in range(heads):
        qo_copy(0, 0, h).start()

    base = me * rows
    q_pos = base + lax.broadcasted_iota(jnp.int32, (rows, 128), 0)
    first = jnp.zeros((rows, 128), jnp.int32)
    for g in range(offs.shape[1]):
        starts = jnp.broadcast_to(offs[0, g : g + 1, :], (rows, 128))
        later = jnp.broadcast_to(offs[1, g : g + 1, :], (rows, 128))
        first = jnp.maximum(first, jnp.where(later <= q_pos, starts, 0))
    first = (first - base).astype(F32)
    low = jnp.max(first.T, axis=0, keepdims=True)
    stats[...] = jnp.zeros(stats.shape, F32)
    stats[2 * heads : 2 * heads + 1, :] = low

    def w_block(index):
        return w_ref[:, pl.ds(pl.multiple_of(index * feats, feats), feats)]

    def relay_kv(h):
        for a in range(2):
            kv_copy(0, a, h).wait_recv()
            kv_copy(1, a, h).start()
        if h + 2 < heads:
            for a in range(2):
                kv_copy(0, a, h + 2).start()

    def relay_qo(a, h):
        qo_copy(0, a, h).wait_recv()
        qo_copy(1, a, h).start()

    loads[0].wait()
    loads[1].wait()
    grad = dot_nt(cot[0], w_block(grp))
    cot_core.wait_recv()
    grad += dot_nt(cot[1], w_block(core_mate))
    relay_kv(0)
    cot_x.wait_recv()
    cot_relay.start()
    grad += dot_nt(cot[2], w_block(x_mate))
    relay_kv(1)
    cot_relay.wait_recv()
    grad += dot_nt(cot[3], w_block(x_core_mate))
    for h in range(heads):
        own_do[h] = grad[:, h * HD : (h + 1) * HD].astype(BF16)
        qo_copy(0, 1, h).start()
    for h in range(heads):
        relay_qo(0, h)
    for copy in head_loads:
        copy.wait()

    key_row = lax.broadcasted_iota(jnp.int32, (rows, rows), 0).astype(F32)
    query_col = lax.broadcasted_iota(jnp.int32, (rows, rows), 1).astype(F32)

    def query_side(h):
        query = own_q[h]
        grad_o = own_do[h]
        key_tiles = (own_k[h], kv[0, 0, h], kv[1, 0, h])
        value_tiles = (own_v[h], kv[0, 1, h], kv[1, 1, h])
        scores = []
        for d in range(3):
            mask = key_row >= low + float(d * rows)
            if d == 0:
                mask = mask & (key_row <= query_col)
            raw = dot_nt(key_tiles[d], query) * scale2
            scores.append(jnp.where(mask, raw, NEG_FILL))
        top = functools.reduce(jnp.maximum, [jnp.max(s, axis=0, keepdims=True) for s in scores])
        expd = [jnp.exp2(s - top) for s in scores]
        total = functools.reduce(jnp.add, [jnp.sum(e, axis=0, keepdims=True) for e in expd])
        inverse = 1.0 / total
        probs = [e * inverse for e in expd]
        probs_b = [p.astype(BF16) for p in probs]
        mixed_t = sum(dot_tn(value_tiles[d], probs_b[d]) for d in range(3))
        attended = mixed_t.T.astype(BF16)
        att[:, h * HD : (h + 1) * HD] = attended
        product = grad_o.astype(F32) * attended.astype(F32)
        delta = jnp.sum(product.T, axis=0, keepdims=True)
        stats[h : h + 1, :] = top + jnp.log2(total)
        stats[heads + h : heads + h + 1, :] = delta
        grads_b = []
        for d in range(3):
            grad_p = dot_nt(value_tiles[d], grad_o)
            grads_b.append((scale * probs[d] * (grad_p - delta)).astype(BF16))
        dq_t = sum(dot_tn(key_tiles[d], grads_b[d]) for d in range(3))
        out_v[0, :, h * HD : (h + 1) * HD] = dq_t.T.astype(BF16)
        acc[0, h] = dot_nn(grads_b[0], query)
        acc[1, h] = dot_nn(probs_b[0], grad_o)

    def key_side(h):
        grad_k = acc[0, h]
        grad_v = acc[1, h]
        for d in range(2):
            query = qo[d, 0, h]
            grad_o = qo[d, 1, h]
            far_low = stats_in[d, 2 * heads : 2 * heads + 1, :] + float((d + 1) * rows)
            log_total = stats_in[d, h : h + 1, :]
            delta = stats_in[d, heads + h : heads + h + 1, :]
            raw = dot_nt(own_k[h], query) * scale2
            probs = jnp.where(key_row >= far_low, jnp.exp2(raw - log_total), 0.0)
            grad_v += dot_nn(probs.astype(BF16), grad_o)
            grad_p = dot_nt(own_v[h], grad_o)
            grad_k += dot_nn((scale * probs * (grad_p - delta)).astype(BF16), query)
        out_v[1, :, h * HD : (h + 1) * HD] = grad_k.astype(BF16)
        out_v[2, :, h * HD : (h + 1) * HD] = grad_v.astype(BF16)

    def wait_far_kv(h):
        for a in range(2):
            kv_copy(1, a, h).wait_recv()

    relay_kv(2)
    wait_far_kv(0)
    query_side(0)
    relay_kv(3)
    relay_qo(1, 0)
    wait_far_kv(1)
    query_side(1)
    relay_qo(1, 1)
    relay_qo(1, 2)
    wait_far_kv(2)
    query_side(2)
    relay_qo(1, 3)
    wait_far_kv(3)
    query_side(3)

    stat_copies = [
        remote(stats, stats_in.at[d], st_send.at[d], st_recv.at[d], (target, grp))
        for d, target in enumerate((left, left2))
    ]
    for copy in stat_copies:
        copy.start()
    out_dq = pltpu.make_async_copy(out_v.at[0], dq_hbm, out_sem.at[0])
    out_dq.start()

    mix_a = remote(mix_out.at[0], mix_in.at[0], mix_send.at[0], mix_recv.at[0], (me, core_mate))
    mix_c = remote(mix_out.at[1], mix_in.at[1], mix_send.at[1], mix_recv.at[1], (me, core_mate))
    mix_x = remote(mix_out.at[2], mix_in.at[2], mix_send.at[2], mix_recv.at[2], (me, x_mate))
    mix_out[0] = dot_nn(att[...], w_block(x_core_mate)).astype(BF16)
    mix_a.start()
    far_part = dot_nn(att[...], w_block(x_mate))
    mix_a.wait_recv()
    mix_out[2] = (far_part + mix_in[0].astype(F32)).astype(BF16)
    mix_x.start()
    mix_out[1] = dot_nn(att[...], w_block(core_mate)).astype(BF16)
    mix_c.start()

    for copy in stat_copies:
        copy.wait_recv()
    for h in range(heads):
        qo_copy(1, 0, h).wait_recv()
        qo_copy(1, 1, h).wait_recv()
        key_side(h)
    out_dk = pltpu.make_async_copy(out_v.at[1], dk_hbm, out_sem.at[1])
    out_dv = pltpu.make_async_copy(out_v.at[2], dv_hbm, out_sem.at[2])
    out_dk.start()
    out_dv.start()

    own_part = dot_nn(att[...], w_block(grp))
    mix_c.wait_recv()
    own_part += mix_in[1].astype(F32)
    mix_x.wait_recv()
    out_v[3] = (own_part + mix_in[2].astype(F32)).astype(BF16)
    out_mixed = pltpu.make_async_copy(out_v.at[3], mixed_hbm, out_sem.at[3])
    out_mixed.start()

    cot_core.wait_send()
    cot_x.wait_send()
    cot_relay.wait_send()
    for hop in range(2):
        for a in range(2):
            for h in range(heads):
                kv_copy(hop, a, h).wait_send()
                qo_copy(hop, a, h).wait_send()
    for copy in stat_copies + [mix_a, mix_c, mix_x]:
        copy.wait_send()
    for copy in (out_dq, out_dk, out_dv, out_mixed):
        copy.wait()


def per_device(n_ctx, queries, key_rows, value_rows, out_weight, cotangent, offsets):
    rows, feats = queries.shape
    heads = feats // HD
    count = offsets.shape[0]
    groups = -(-count // 128)
    later = jnp.concatenate(
        [offsets[PREV:], jnp.full((groups * 128 - count + PREV,), 2**30, jnp.int32)]
    )
    starts = jnp.concatenate([offsets, jnp.zeros((groups * 128 - count,), jnp.int32)])
    offs = jnp.stack([starts, later]).reshape(2, groups, 128)
    any_spec = pl.BlockSpec(memory_space=pl.ANY)
    tile = jax.ShapeDtypeStruct((rows, feats), BF16)
    dma = pltpu.SemaphoreType.DMA
    outs = pl.pallas_call(
        functools.partial(kernel, n_ctx),
        out_shape=(tile, tile, tile, tile),
        in_specs=[any_spec] * 5 + [pl.BlockSpec(memory_space=pltpu.VMEM)],
        out_specs=(any_spec,) * 4,
        scratch_shapes=[
            pltpu.VMEM((heads, rows, HD), BF16),
            pltpu.VMEM((heads, rows, HD), BF16),
            pltpu.VMEM((heads, rows, HD), BF16),
            pltpu.VMEM((heads, rows, HD), BF16),
            pltpu.VMEM(out_weight.shape, BF16),
            pltpu.VMEM((4, rows, feats), BF16),
            pltpu.VMEM((2, 2, heads, rows, HD), BF16),
            pltpu.VMEM((2, 2, heads, rows, HD), BF16),
            pltpu.VMEM((16, rows), F32),
            pltpu.VMEM((2, 16, rows), F32),
            pltpu.VMEM((rows, feats), BF16),
            pltpu.VMEM((2, heads, rows, HD), F32),
            pltpu.VMEM((3, rows, feats), BF16),
            pltpu.VMEM((3, rows, feats), BF16),
            pltpu.VMEM((4, rows, feats), BF16),
            dma((2 + 3 * heads,)),
            dma((3,)),
            dma((3,)),
            dma((2, 2, heads)),
            dma((2, 2, heads)),
            dma((2, 2, heads)),
            dma((2, 2, heads)),
            dma((2,)),
            dma((2,)),
            dma((3,)),
            dma((3,)),
            dma((4,)),
        ],
        compiler_params=pltpu.CompilerParams(
            collective_id=0, has_side_effects=True, vmem_limit_bytes=48 * 1024 * 1024
        ),
    )(queries, key_rows, value_rows, out_weight, cotangent, offs)
    return outs


def solution(mesh):
    in_specs = (
        P("ctx", "head"),
        P("ctx", "head"),
        P("ctx", "head"),
        P("head", None),
        P("ctx", "head"),
        P(),
    )
    out_specs = (P("ctx", "head"), P("ctx", "head"), P("ctx", "head"), P("ctx", "head"))
    return jax.shard_map(
        functools.partial(per_device, mesh.shape["ctx"]),
        mesh=mesh,
        in_specs=in_specs,
        out_specs=out_specs,
        check_vma=False,
    )
```

```python
import functools
import math

import jax
import jax.numpy as jnp
from jax import lax
from jax.experimental import pallas as pl
from jax.experimental.pallas import tpu as pltpu
from jax.sharding import PartitionSpec as P

HD = 128
PREV = 3
NEG_FILL = -1e30
LOG2E = math.log2(math.e)
F32 = jnp.float32
BF16 = jnp.bfloat16
MESH = pl.DeviceIdType.MESH


def dot_nn(a, b):
    return lax.dot_general(a, b, (((1,), (0,)), ((), ())), preferred_element_type=F32)


def dot_nt(a, b):
    return lax.dot_general(a, b, (((1,), (1,)), ((), ())), preferred_element_type=F32)


def dot_tn(a, b):
    return lax.dot_general(a, b, (((0,), (0,)), ((), ())), preferred_element_type=F32)


def kernel(
    n_ctx, groups, q_hbm, k_hbm, v_hbm, w_hbm, c_hbm, offs,
    out_ref,
    own_q, own_k, own_v, own_do, w_ref, cot, kv, qo, stats, stats_in,
    att, acc, mix_out, mix_in,
    load_sem, cot_send, cot_recv, kv_send, kv_recv, qo_send, qo_recv,
    st_send, st_recv, mix_send, mix_recv,
):
    rows = q_hbm.shape[0]
    feats = q_hbm.shape[1]
    heads = feats // HD
    scale = 1.0 / math.sqrt(HD)
    scale2 = scale * LOG2E
    half = n_ctx // 2
    me = lax.axis_index("ctx")
    grp = lax.axis_index("head")
    first_dev = me == 0
    last_dev = me == n_ctx - 1
    at_end = (me == half - 1).astype(jnp.int32)
    at_start = (me == half).astype(jnp.int32)
    is_last = last_dev.astype(jnp.int32)
    is_first = first_dev.astype(jnp.int32)
    right = me + 1 + at_end * (n_ctx - 1 - half) + is_last * (half - n_ctx)
    left = me - 1 + at_start * (1 - half) + is_first * half
    from_left = me - 1 + at_start * half + is_first * (half + 1)
    from_right = me + 1 - at_end * half + is_last * (half - 1 - n_ctx)
    to_stats = lax.rem(me + n_ctx - 1, n_ctx)
    to_stats2 = lax.rem(me + n_ctx - 2, n_ctx)
    of_stats = lax.rem(me + 1, n_ctx)
    of_stats2 = lax.rem(me + 2, n_ctx)
    core = lax.rem(grp, 2)
    pair = grp // 2
    core_mate = pair * 2 + (1 - core)
    x_mate = (1 - pair) * 2 + core
    x_core_mate = (1 - pair) * 2 + (1 - core)

    barrier = pltpu.get_barrier_semaphore()
    senders = (
        (from_left, grp), (from_right, grp), (of_stats, grp), (of_stats2, grp),
        (me, core_mate), (me, x_mate),
    )
    for target in senders:
        pl.semaphore_signal(barrier, inc=1, device_id=target, device_id_type=MESH)

    def cols(ref, h):
        return ref.at[:, h * HD : (h + 1) * HD]

    loads = []
    for slot, (src, dst) in enumerate(((c_hbm, cot.at[0]), (w_hbm, w_ref))):
        loads.append(pltpu.make_async_copy(src, dst, load_sem.at[slot]))
    head_loads = []
    for a, (src, dst) in enumerate(((q_hbm, own_q), (k_hbm, own_k), (v_hbm, own_v))):
        for h in range(heads):
            head_loads.append(
                pltpu.make_async_copy(cols(src, h), dst.at[h], load_sem.at[2 + a * heads + h])
            )
    for copy in loads + head_loads:
        copy.start()

    def remote(src, dst, send, recv, target):
        return pltpu.make_async_remote_copy(
            src_ref=src, dst_ref=dst, send_sem=send, recv_sem=recv,
            device_id=target, device_id_type=MESH,
        )

    def kv_copy(hop, a, h, src=None):
        slot = hop + 2 * at_end
        return remote(
            kv.at[0, a, h] if src is None else src, kv.at[slot, a, h],
            kv_send.at[hop, a, h], kv_recv.at[slot, a, h], (right, grp),
        )

    def qo_copy(hop, a, h, src=None):
        slot = hop + 2 * at_start
        return remote(
            qo.at[0, a, h] if src is None else src, qo.at[slot, a, h],
            qo_send.at[hop, a, h], qo_recv.at[slot, a, h], (left, grp),
        )

    def arrived(buf, sems, slot, a, h):
        part, sem = buf.at[slot, a, h], sems.at[slot, a, h]
        remote(part, part, sem, sem, (me, core_mate)).wait_recv()

    def send_own_kv(h):
        @pl.when(jnp.logical_not(last_dev))
        def _():
            kv_copy(0, 0, h, cols(k_hbm, h)).start()
            kv_copy(0, 1, h, cols(v_hbm, h)).start()

    def send_own_qo(a, h):
        @pl.when(jnp.logical_not(first_dev))
        def _():
            qo_copy(0, a, h, cols(q_hbm, h) if a == 0 else own_do.at[h]).start()

    def relay_kv(h):
        for a in range(2):
            @pl.when(jnp.logical_not(first_dev))
            def _():
                arrived(kv, kv_recv, 0, a, h)

            @pl.when((me > 0) & (me < n_ctx - 1))
            def _():
                kv_copy(1, a, h).start()

            @pl.when(last_dev)
            def _():
                arrived(kv, kv_recv, 2, a, h)
                kv_copy(0, a, h, kv.at[2, a, h]).start()

    def wait_far_kv(h):
        for a in range(2):
            @pl.when(me > 1)
            def _():
                arrived(kv, kv_recv, 1, a, h)

            @pl.when(last_dev)
            def _():
                arrived(kv, kv_recv, 3, a, h)
                kv_copy(1, a, h, kv.at[3, a, h]).start()

    def relay_qo(a, h):
        @pl.when(jnp.logical_not(last_dev))
        def _():
            arrived(qo, qo_recv, 0, a, h)

        @pl.when((me > 0) & (me < n_ctx - 1))
        def _():
            qo_copy(1, a, h).start()

        @pl.when(first_dev)
        def _():
            arrived(qo, qo_recv, 2, a, h)
            qo_copy(0, a, h, qo.at[2, a, h]).start()

    def forward_far_qo(a, h):
        @pl.when(first_dev)
        def _():
            arrived(qo, qo_recv, 3, a, h)
            qo_copy(1, a, h, qo.at[3, a, h]).start()

    def wait_far_qo(h):
        for a in range(2):
            @pl.when(me < n_ctx - 2)
            def _():
                arrived(qo, qo_recv, 1, a, h)

    cot_core = remote(c_hbm, cot.at[1], cot_send.at[0], cot_recv.at[0], (me, core_mate))
    cot_x = remote(c_hbm, cot.at[2], cot_send.at[1], cot_recv.at[1], (me, x_mate))
    cot_relay = remote(cot.at[2], cot.at[3], cot_send.at[2], cot_recv.at[2], (me, core_mate))

    pl.semaphore_wait(barrier, 6)
    cot_x.start()
    cot_core.start()
    for h in range(heads):
        send_own_qo(0, h)
        send_own_kv(h)

    @pl.when(first_dev)
    def _():
        kv[0] = jnp.zeros(kv.shape[1:], BF16)

    @pl.when(me <= 1)
    def _():
        kv[1] = jnp.zeros(kv.shape[1:], BF16)

    @pl.when(last_dev)
    def _():
        qo[0] = jnp.zeros(qo.shape[1:], BF16)

    @pl.when(me >= n_ctx - 2)
    def _():
        qo[1] = jnp.zeros(qo.shape[1:], BF16)

    base = me * rows
    q_pos = base + lax.broadcasted_iota(jnp.int32, (rows, 128), 0)
    first = jnp.zeros((rows, 128), jnp.int32)
    lists = offs[...]
    turned = pltpu.roll(lists, 128 - PREV, 1)
    lane = lax.broadcasted_iota(jnp.int32, lists.shape, 1)
    ahead = jnp.where(lane < 128 - PREV, turned, pltpu.roll(turned, lists.shape[0] - 1, 0))
    for g in range(groups):
        starts = jnp.broadcast_to(lists[g : g + 1, :], (rows, 128))
        later = jnp.broadcast_to(ahead[g : g + 1, :], (rows, 128))
        first = jnp.maximum(first, jnp.where(later <= q_pos, starts, 0))
    first = (first - base).astype(F32)
    low = jnp.max(first.T, axis=0, keepdims=True)
    stats[...] = jnp.zeros(stats.shape, F32)
    stats[2 * heads : 2 * heads + 1, :] = low

    def w_block(index):
        return w_ref[:, pl.ds(pl.multiple_of(index * feats, feats), feats)]

    loads[0].wait()
    loads[1].wait()
    grad = dot_nt(cot[0], w_block(grp))
    cot_core.wait_recv()
    grad += dot_nt(cot[1], w_block(core_mate))
    for h in range(heads):
        relay_qo(0, h)
    relay_kv(0)
    cot_x.wait_recv()
    cot_relay.start()
    grad += dot_nt(cot[2], w_block(x_mate))
    relay_kv(1)
    cot_relay.wait_recv()
    grad += dot_nt(cot[3], w_block(x_core_mate))
    for h in range(heads):
        own_do[h] = grad[:, h * HD : (h + 1) * HD].astype(BF16)
        send_own_qo(1, h)
    for copy in head_loads:
        copy.wait()

    key_row = lax.broadcasted_iota(jnp.int32, (rows, rows), 0).astype(F32)
    query_col = lax.broadcasted_iota(jnp.int32, (rows, rows), 1).astype(F32)

    def query_side(h):
        query = own_q[h]
        grad_o = own_do[h]
        key_tiles = (own_k[h], kv[0, 0, h], kv[1, 0, h])
        value_tiles = (own_v[h], kv[0, 1, h], kv[1, 1, h])
        scores = []
        for d in range(3):
            mask = key_row >= low + float(d * rows)
            if d == 0:
                mask = mask & (key_row <= query_col)
            raw = dot_nt(key_tiles[d], query) * scale2
            scores.append(jnp.where(mask, raw, NEG_FILL))
        top = functools.reduce(jnp.maximum, [jnp.max(s, axis=0, keepdims=True) for s in scores])
        expd = [jnp.exp2(s - top) for s in scores]
        total = functools.reduce(jnp.add, [jnp.sum(e, axis=0, keepdims=True) for e in expd])
        inverse = 1.0 / total
        probs = [e * inverse for e in expd]
        probs_b = [p.astype(BF16) for p in probs]
        mixed_t = sum(dot_tn(value_tiles[d], probs_b[d]) for d in range(3))
        attended = mixed_t.T.astype(BF16)
        att[:, h * HD : (h + 1) * HD] = attended
        product = grad_o.astype(F32) * attended.astype(F32)
        delta = jnp.sum(product.T, axis=0, keepdims=True)
        stats[h : h + 1, :] = top + jnp.log2(total)
        stats[heads + h : heads + h + 1, :] = delta
        grads_b = []
        for d in range(3):
            grad_p = dot_nt(value_tiles[d], grad_o)
            grads_b.append((scale * probs[d] * (grad_p - delta)).astype(BF16))
        dq_t = sum(dot_tn(key_tiles[d], grads_b[d]) for d in range(3))
        out_ref[1, :, h * HD : (h + 1) * HD] = dq_t.T.astype(BF16)
        acc[0, h] = dot_nn(grads_b[0], query)
        acc[1, h] = dot_nn(probs_b[0], grad_o)

    def key_side(h):
        grad_k = acc[0, h]
        grad_v = acc[1, h]
        for d in range(2):
            query = qo[d, 0, h]
            grad_o = qo[d, 1, h]
            far_low = stats_in[d, 2 * heads : 2 * heads + 1, :] + float((d + 1) * rows)
            log_total = stats_in[d, h : h + 1, :]
            delta = stats_in[d, heads + h : heads + h + 1, :]
            raw = dot_nt(own_k[h], query) * scale2
            probs = jnp.where(key_row >= far_low, jnp.exp2(raw - log_total), 0.0)
            grad_v += dot_nn(probs.astype(BF16), grad_o)
            grad_p = dot_nt(own_v[h], grad_o)
            grad_k += dot_nn((scale * probs * (grad_p - delta)).astype(BF16), query)
        out_ref[2, :, h * HD : (h + 1) * HD] = grad_k.astype(BF16)
        out_ref[3, :, h * HD : (h + 1) * HD] = grad_v.astype(BF16)

    relay_kv(2)
    for h in range(heads):
        forward_far_qo(0, h)
    relay_kv(3)
    wait_far_kv(0)
    query_side(0)
    relay_qo(1, 0)
    relay_qo(1, 1)
    wait_far_kv(1)
    forward_far_qo(1, 0)
    query_side(1)
    relay_qo(1, 2)
    relay_qo(1, 3)
    wait_far_kv(2)
    forward_far_qo(1, 1)
    query_side(2)
    wait_far_kv(3)
    forward_far_qo(1, 2)
    query_side(3)
    forward_far_qo(1, 3)

    stat_copies = [
        remote(stats, stats_in.at[d], st_send.at[d], st_recv.at[d], (target, grp))
        for d, target in enumerate((to_stats, to_stats2))
    ]
    for copy in stat_copies:
        copy.start()

    mix_a = remote(mix_out.at[0], mix_in.at[0], mix_send.at[0], mix_recv.at[0], (me, core_mate))
    mix_c = remote(mix_out.at[1], mix_in.at[1], mix_send.at[1], mix_recv.at[1], (me, core_mate))
    mix_x = remote(mix_out.at[2], mix_in.at[2], mix_send.at[2], mix_recv.at[2], (me, x_mate))
    mix_out[0] = dot_nn(att[...], w_block(x_core_mate)).astype(BF16)
    mix_a.start()
    far_part = dot_nn(att[...], w_block(x_mate))
    mix_a.wait_recv()
    mix_out[2] = (far_part + mix_in[0].astype(F32)).astype(BF16)
    mix_x.start()
    mix_out[1] = dot_nn(att[...], w_block(core_mate)).astype(BF16)
    mix_c.start()

    for copy in stat_copies:
        copy.wait_recv()
    for h in range(heads):
        wait_far_qo(h)
        key_side(h)

    own_part = dot_nn(att[...], w_block(grp))
    mix_c.wait_recv()
    own_part += mix_in[1].astype(F32)
    mix_x.wait_recv()
    out_ref[0] = (own_part + mix_in[2].astype(F32)).astype(BF16)

    cot_core.wait_send()
    cot_x.wait_send()
    cot_relay.wait_send()
    for a in range(2):
        for h in range(heads):
            kv_copy(0, a, h).wait_send()
            qo_copy(0, a, h).wait_send()

            @pl.when(jnp.logical_not(first_dev))
            def _():
                kv_copy(1, a, h).wait_send()

            @pl.when(jnp.logical_not(last_dev))
            def _():
                qo_copy(1, a, h).wait_send()
    for copy in stat_copies + [mix_a, mix_c, mix_x]:
        copy.wait_send()


def spread(all_ref, *refs):
    outs, sems = refs[:-1], refs[-1]
    copies = [
        pltpu.make_async_copy(all_ref.at[i], out, sems.at[i]) for i, out in enumerate(outs)
    ]
    for copy in copies:
        copy.start()
    for copy in copies:
        copy.wait()


def per_device(n_ctx, queries, key_rows, value_rows, out_weight, cotangent, offsets):
    rows, feats = queries.shape
    heads = feats // HD
    count = offsets.shape[0]
    groups = -(-count // 128)
    padded = -(-(groups + 1) // 8) * 8
    offs = jnp.pad(offsets, (0, padded * 128 - count), constant_values=2**30)
    offs = offs.reshape(padded, 128)
    any_spec = pl.BlockSpec(memory_space=pl.ANY)
    vmem_spec = pl.BlockSpec(memory_space=pltpu.VMEM)
    tile = jax.ShapeDtypeStruct((rows, feats), BF16)
    dma = pltpu.SemaphoreType.DMA
    four = pl.pallas_call(
        functools.partial(kernel, n_ctx, groups),
        out_shape=jax.ShapeDtypeStruct((4, rows, feats), BF16),
        in_specs=[any_spec] * 5 + [vmem_spec],
        out_specs=vmem_spec,
        scratch_shapes=[
            pltpu.VMEM((heads, rows, HD), BF16),
            pltpu.VMEM((heads, rows, HD), BF16),
            pltpu.VMEM((heads, rows, HD), BF16),
            pltpu.VMEM((heads, rows, HD), BF16),
            pltpu.VMEM(out_weight.shape, BF16),
            pltpu.VMEM((4, rows, feats), BF16),
            pltpu.VMEM((4, 2, heads, rows, HD), BF16),
            pltpu.VMEM((4, 2, heads, rows, HD), BF16),
            pltpu.VMEM((16, rows), F32),
            pltpu.VMEM((2, 16, rows), F32),
            pltpu.VMEM((rows, feats), BF16),
            pltpu.VMEM((2, heads, rows, HD), F32),
            pltpu.VMEM((3, rows, feats), BF16),
            pltpu.VMEM((3, rows, feats), BF16),
            dma((2 + 3 * heads,)),
            dma((3,)),
            dma((3,)),
            dma((2, 2, heads)),
            dma((4, 2, heads)),
            dma((2, 2, heads)),
            dma((4, 2, heads)),
            dma((2,)),
            dma((2,)),
            dma((3,)),
            dma((3,)),
        ],
        compiler_params=pltpu.CompilerParams(
            collective_id=0, has_side_effects=True, vmem_limit_bytes=58 * 1024 * 1024
        ),
    )(queries, key_rows, value_rows, out_weight, cotangent, offs)
    return pl.pallas_call(
        spread,
        out_shape=(tile,) * 4,
        in_specs=[any_spec],
        out_specs=(any_spec,) * 4,
        scratch_shapes=[dma((4,))],
    )(four)


def solution(mesh):
    in_specs = (
        P("ctx", "head"),
        P("ctx", "head"),
        P("ctx", "head"),
        P("head", None),
        P("ctx", "head"),
        P(),
    )
    out_specs = (P("ctx", "head"), P("ctx", "head"), P("ctx", "head"), P("ctx", "head"))
    return jax.shard_map(
        functools.partial(per_device, mesh.shape["ctx"]),
        mesh=mesh,
        in_specs=in_specs,
        out_specs=out_specs,
        check_vma=False,
    )
```

```python
import functools
import math

import jax
import jax.numpy as jnp
from jax import lax
from jax.experimental import pallas as pl
from jax.experimental.pallas import tpu as pltpu
from jax.sharding import PartitionSpec as P

HD = 128
PREV = 3
NEG_FILL = -1e30
LOG2E = math.log2(math.e)
F32 = jnp.float32
BF16 = jnp.bfloat16
MESH = pl.DeviceIdType.MESH


def dot_nn(a, b):
    return lax.dot_general(a, b, (((1,), (0,)), ((), ())), preferred_element_type=F32)


def dot_nt(a, b):
    return lax.dot_general(a, b, (((1,), (1,)), ((), ())), preferred_element_type=F32)


def dot_tn(a, b):
    return lax.dot_general(a, b, (((0,), (0,)), ((), ())), preferred_element_type=F32)


def kernel(
    n_ctx, groups, q_hbm, k_hbm, v_hbm, w_hbm, c_hbm, offs,
    out_ref,
    own_q, own_k, own_v, own_do, w_ref, cot, kv, qo, stats, stats_in,
    att, acc, mix_out, mix_in,
    load_sem, cot_send, cot_recv, kv_send, kv_recv, qo_send, qo_recv,
    st_send, st_recv, mix_send, mix_recv,
):
    rows = q_hbm.shape[0]
    feats = q_hbm.shape[1]
    heads = feats // HD
    scale = 1.0 / math.sqrt(HD)
    scale2 = scale * LOG2E
    half = n_ctx // 2
    me = lax.axis_index("ctx")
    grp = lax.axis_index("head")
    first_dev = me == 0
    last_dev = me == n_ctx - 1
    end_dev = me == half - 1
    start_dev = me == half
    at_end = end_dev.astype(jnp.int32)
    at_start = start_dev.astype(jnp.int32)
    is_last = last_dev.astype(jnp.int32)
    is_first = first_dev.astype(jnp.int32)
    key_right = me + 1 + at_end * (n_ctx - 1 - half) + is_last * (half - n_ctx)
    query_left = me - 1 + at_start * (1 - half) + is_first * half
    greet_left = me - 1 + is_first * (half + 1)
    greet_right = me + 1 + is_last * (half - 1 - n_ctx)
    to_stats = lax.rem(me + n_ctx - 1, n_ctx)
    to_stats2 = lax.rem(me + n_ctx - 2, n_ctx)
    of_stats = lax.rem(me + 1, n_ctx)
    of_stats2 = lax.rem(me + 2, n_ctx)
    core = lax.rem(grp, 2)
    pair = grp // 2
    core_mate = pair * 2 + (1 - core)
    x_mate = (1 - pair) * 2 + core
    x_core_mate = (1 - pair) * 2 + (1 - core)

    barrier = pltpu.get_barrier_semaphore()
    senders = (
        (greet_left, grp), (greet_right, grp), (of_stats, grp), (of_stats2, grp),
        (me, core_mate), (me, x_mate),
    )
    for target in senders:
        pl.semaphore_signal(barrier, inc=1, device_id=target, device_id_type=MESH)

    @pl.when(end_dev)
    def _():
        pl.semaphore_signal(barrier, inc=1, device_id=(0, grp), device_id_type=MESH)

    @pl.when(start_dev)
    def _():
        pl.semaphore_signal(barrier, inc=1, device_id=(n_ctx - 1, grp), device_id_type=MESH)

    def cols(ref, h):
        return ref.at[:, h * HD : (h + 1) * HD]

    loads = []
    for slot, (src, dst) in enumerate(((c_hbm, cot.at[0]), (w_hbm, w_ref))):
        loads.append(pltpu.make_async_copy(src, dst, load_sem.at[slot]))
    head_loads = []
    for a, (src, dst) in enumerate(((q_hbm, own_q), (k_hbm, own_k), (v_hbm, own_v))):
        for h in range(heads):
            head_loads.append(
                pltpu.make_async_copy(cols(src, h), dst.at[h], load_sem.at[2 + a * heads + h])
            )
    for copy in loads + head_loads:
        copy.start()

    def remote(src, dst, send, recv, target):
        return pltpu.make_async_remote_copy(
            src_ref=src, dst_ref=dst, send_sem=send, recv_sem=recv,
            device_id=target, device_id_type=MESH,
        )

    def kv_copy(hop, a, h, src=None):
        slot = hop + 2 * at_end if a == 0 else hop
        return remote(
            kv.at[0, a, h] if src is None else src, kv.at[slot, a, h],
            kv_send.at[hop, a, h], kv_recv.at[slot, a, h],
            (key_right if a == 0 else me + 1, grp),
        )

    def qo_copy(hop, a, h, src=None):
        slot = hop + 2 * at_start if a == 0 else hop
        return remote(
            qo.at[0, a, h] if src is None else src, qo.at[slot, a, h],
            qo_send.at[hop, a, h], qo_recv.at[slot, a, h],
            (query_left if a == 0 else me - 1, grp),
        )

    def arrived(buf, sems, slot, a, h):
        part, sem = buf.at[slot, a, h], sems.at[slot, a, h]
        remote(part, part, sem, sem, (me, core_mate)).wait_recv()

    not_first = jnp.logical_not(first_dev)
    not_last = jnp.logical_not(last_dev)
    inner = (me > 0) & (me < n_ctx - 1)

    def send_own_kv(h):
        @pl.when(not_last)
        def _():
            kv_copy(0, 0, h, cols(k_hbm, h)).start()
            kv_copy(0, 1, h, cols(v_hbm, h)).start()

    def send_own_qo(a, h):
        @pl.when(not_first)
        def _():
            qo_copy(0, a, h, cols(q_hbm, h) if a == 0 else own_do.at[h]).start()

    def relay_kv(h):
        for a in range(2):
            @pl.when(not_first)
            def _():
                arrived(kv, kv_recv, 0, a, h)

            @pl.when(inner)
            def _():
                kv_copy(1, a, h).start()

    def wait_far_kv(h):
        for a in range(2):
            @pl.when(me > 1)
            def _():
                arrived(kv, kv_recv, 1, a, h)

    def forward_keys(hop, h):
        @pl.when(last_dev)
        def _():
            arrived(kv, kv_recv, hop + 2, 0, h)
            kv_copy(hop, 0, h, kv.at[hop + 2, 0, h]).start()

    def forward_queries(hop, h):
        @pl.when(first_dev)
        def _():
            arrived(qo, qo_recv, hop + 2, 0, h)
            qo_copy(hop, 0, h, qo.at[hop + 2, 0, h]).start()

    def relay_qo(a, h):
        arrived(qo, qo_recv, 0, a, h)

        @pl.when(me > 0)
        def _():
            qo_copy(1, a, h).start()

    def wait_far_qo(h):
        for a in range(2):
            @pl.when(me < n_ctx - 2)
            def _():
                arrived(qo, qo_recv, 1, a, h)

    def relay_do(h):
        @pl.when(not_last)
        def _():
            relay_qo(1, h)

    cot_core = remote(c_hbm, cot.at[1], cot_send.at[0], cot_recv.at[0], (me, core_mate))
    cot_x = remote(c_hbm, cot.at[2], cot_send.at[1], cot_recv.at[1], (me, x_mate))
    cot_relay = remote(cot.at[2], cot.at[3], cot_send.at[2], cot_recv.at[2], (me, core_mate))

    pl.semaphore_wait(barrier, 6 + at_end + at_start)
    cot_x.start()
    cot_core.start()
    for h in range(heads):
        send_own_qo(0, h)
        send_own_kv(h)

    @pl.when(first_dev)
    def _():
        kv[0] = jnp.zeros(kv.shape[1:], BF16)

    @pl.when(me <= 1)
    def _():
        kv[1] = jnp.zeros(kv.shape[1:], BF16)

    @pl.when(last_dev)
    def _():
        qo[0] = jnp.zeros(qo.shape[1:], BF16)

    @pl.when(me >= n_ctx - 2)
    def _():
        qo[1] = jnp.zeros(qo.shape[1:], BF16)

    base = me * rows
    q_pos = base + lax.broadcasted_iota(jnp.int32, (rows, 128), 0)
    first = jnp.zeros((rows, 128), jnp.int32)
    lists = offs[...]
    turned = pltpu.roll(lists, 128 - PREV, 1)
    lane = lax.broadcasted_iota(jnp.int32, lists.shape, 1)
    ahead = jnp.where(lane < 128 - PREV, turned, pltpu.roll(turned, lists.shape[0] - 1, 0))
    for g in range(groups):
        starts = jnp.broadcast_to(lists[g : g + 1, :], (rows, 128))
        later = jnp.broadcast_to(ahead[g : g + 1, :], (rows, 128))
        first = jnp.maximum(first, jnp.where(later <= q_pos, starts, 0))
    first = (first - base).astype(F32)
    low = jnp.max(first.T, axis=0, keepdims=True)
    stats[...] = jnp.zeros(stats.shape, F32)
    stats[2 * heads : 2 * heads + 1, :] = low

    def w_block(index):
        return w_ref[:, pl.ds(pl.multiple_of(index * feats, feats), feats)]

    loads[0].wait()
    loads[1].wait()
    grad = dot_nt(cot[0], w_block(grp))
    cot_core.wait_recv()
    grad += dot_nt(cot[1], w_block(core_mate))

    @pl.when(not_last & jnp.logical_not(end_dev))
    def _():
        for h in range(heads):
            relay_qo(0, h)

    cot_x.wait_recv()
    cot_relay.start()
    grad += dot_nt(cot[2], w_block(x_mate))
    cot_relay.wait_recv()
    grad += dot_nt(cot[3], w_block(x_core_mate))
    for h in range(heads):
        own_do[h] = grad[:, h * HD : (h + 1) * HD].astype(BF16)
        send_own_qo(1, h)
    for h in range(heads):
        forward_queries(0, h)
    for h in range(3):
        relay_kv(h)
        forward_keys(0, h)
    for copy in head_loads:
        copy.wait()

    key_row = lax.broadcasted_iota(jnp.int32, (rows, rows), 0).astype(F32)
    query_col = lax.broadcasted_iota(jnp.int32, (rows, rows), 1).astype(F32)

    def query_side(h):
        query = own_q[h]
        grad_o = own_do[h]
        key_tiles = (own_k[h], kv[0, 0, h], kv[1, 0, h])
        value_tiles = (own_v[h], kv[0, 1, h], kv[1, 1, h])
        scores = []
        for d in range(3):
            mask = key_row >= low + float(d * rows)
            if d == 0:
                mask = mask & (key_row <= query_col)
            raw = dot_nt(key_tiles[d], query) * scale2
            scores.append(jnp.where(mask, raw, NEG_FILL))
        top = functools.reduce(jnp.maximum, [jnp.max(s, axis=0, keepdims=True) for s in scores])
        expd = [jnp.exp2(s - top) for s in scores]
        total = functools.reduce(jnp.add, [jnp.sum(e, axis=0, keepdims=True) for e in expd])
        inverse = 1.0 / total
        probs = [e * inverse for e in expd]
        probs_b = [p.astype(BF16) for p in probs]
        mixed_t = sum(dot_tn(value_tiles[d], probs_b[d]) for d in range(3))
        attended = mixed_t.T.astype(BF16)
        att[:, h * HD : (h + 1) * HD] = attended
        product = grad_o.astype(F32) * attended.astype(F32)
        delta = jnp.sum(product.T, axis=0, keepdims=True)
        stats[h : h + 1, :] = top + jnp.log2(total)
        stats[heads + h : heads + h + 1, :] = delta
        grads_b = []
        for d in range(3):
            grad_p = dot_nt(value_tiles[d], grad_o)
            grads_b.append((scale * probs[d] * (grad_p - delta)).astype(BF16))
        dq_t = sum(dot_tn(key_tiles[d], grads_b[d]) for d in range(3))
        out_ref[1, :, h * HD : (h + 1) * HD] = dq_t.T.astype(BF16)
        acc[0, h] = dot_nn(grads_b[0], query)
        acc[1, h] = dot_nn(probs_b[0], grad_o)

    def key_side(h):
        grad_k = acc[0, h]
        grad_v = acc[1, h]
        for d in range(2):
            query = qo[d, 0, h]
            grad_o = qo[d, 1, h]
            far_low = stats_in[d, 2 * heads : 2 * heads + 1, :] + float((d + 1) * rows)
            log_total = stats_in[d, h : h + 1, :]
            delta = stats_in[d, heads + h : heads + h + 1, :]
            raw = dot_nt(own_k[h], query) * scale2
            probs = jnp.where(key_row >= far_low, jnp.exp2(raw - log_total), 0.0)
            grad_v += dot_nn(probs.astype(BF16), grad_o)
            grad_p = dot_nt(own_v[h], grad_o)
            grad_k += dot_nn((scale * probs * (grad_p - delta)).astype(BF16), query)
        out_ref[2, :, h * HD : (h + 1) * HD] = grad_k.astype(BF16)
        out_ref[3, :, h * HD : (h + 1) * HD] = grad_v.astype(BF16)

    for h in range(heads):
        forward_queries(1, h)

    relay_kv(3)
    forward_keys(0, 3)

    @pl.when(end_dev)
    def _():
        for h in range(heads):
            relay_qo(0, h)

    for h in range(3):
        forward_keys(1, h)
    wait_far_kv(0)
    query_side(0)
    relay_do(0)
    relay_do(1)
    forward_keys(1, 3)
    wait_far_kv(1)
    query_side(1)
    relay_do(2)
    relay_do(3)
    wait_far_kv(2)
    query_side(2)
    wait_far_kv(3)
    query_side(3)

    stat_copies = [
        remote(stats, stats_in.at[d], st_send.at[d], st_recv.at[d], (target, grp))
        for d, target in enumerate((to_stats, to_stats2))
    ]
    for copy in stat_copies:
        copy.start()

    mix_a = remote(mix_out.at[0], mix_in.at[0], mix_send.at[0], mix_recv.at[0], (me, core_mate))
    mix_c = remote(mix_out.at[1], mix_in.at[1], mix_send.at[1], mix_recv.at[1], (me, core_mate))
    mix_x = remote(mix_out.at[2], mix_in.at[2], mix_send.at[2], mix_recv.at[2], (me, x_mate))
    mix_out[0] = dot_nn(att[...], w_block(x_core_mate)).astype(BF16)
    mix_a.start()
    far_part = dot_nn(att[...], w_block(x_mate))
    mix_a.wait_recv()
    mix_out[2] = (far_part + mix_in[0].astype(F32)).astype(BF16)
    mix_x.start()
    mix_out[1] = dot_nn(att[...], w_block(core_mate)).astype(BF16)
    mix_c.start()

    for copy in stat_copies:
        copy.wait_recv()
    for h in range(heads):
        wait_far_qo(h)
        key_side(h)

    own_part = dot_nn(att[...], w_block(grp))
    mix_c.wait_recv()
    own_part += mix_in[1].astype(F32)
    mix_x.wait_recv()
    out_ref[0] = (own_part + mix_in[2].astype(F32)).astype(BF16)

    cot_core.wait_send()
    cot_x.wait_send()
    cot_relay.wait_send()
    for h in range(heads):
        kv_copy(0, 0, h).wait_send()
        qo_copy(0, 0, h).wait_send()

        @pl.when(not_last)
        def _():
            kv_copy(0, 1, h).wait_send()
            qo_copy(1, 0, h).wait_send()

        @pl.when(not_first)
        def _():
            qo_copy(0, 1, h).wait_send()
            kv_copy(1, 0, h).wait_send()

        @pl.when(inner)
        def _():
            kv_copy(1, 1, h).wait_send()
            qo_copy(1, 1, h).wait_send()

    for copy in stat_copies + [mix_a, mix_c, mix_x]:
        copy.wait_send()


def spread(all_ref, *refs):
    outs, sems = refs[:-1], refs[-1]
    copies = [
        pltpu.make_async_copy(all_ref.at[i], out, sems.at[i]) for i, out in enumerate(outs)
    ]
    for copy in copies:
        copy.start()
    for copy in copies:
        copy.wait()


def per_device(n_ctx, queries, key_rows, value_rows, out_weight, cotangent, offsets):
    rows, feats = queries.shape
    heads = feats // HD
    count = offsets.shape[0]
    groups = -(-count // 128)
    padded = -(-(groups + 1) // 8) * 8
    offs = jnp.pad(offsets, (0, padded * 128 - count), constant_values=2**30)
    offs = offs.reshape(padded, 128)
    any_spec = pl.BlockSpec(memory_space=pl.ANY)
    vmem_spec = pl.BlockSpec(memory_space=pltpu.VMEM)
    tile = jax.ShapeDtypeStruct((rows, feats), BF16)
    dma = pltpu.SemaphoreType.DMA
    four = pl.pallas_call(
        functools.partial(kernel, n_ctx, groups),
        out_shape=jax.ShapeDtypeStruct((4, rows, feats), BF16),
        in_specs=[any_spec] * 5 + [vmem_spec],
        out_specs=vmem_spec,
        scratch_shapes=[
            pltpu.VMEM((heads, rows, HD), BF16),
            pltpu.VMEM((heads, rows, HD), BF16),
            pltpu.VMEM((heads, rows, HD), BF16),
            pltpu.VMEM((heads, rows, HD), BF16),
            pltpu.VMEM(out_weight.shape, BF16),
            pltpu.VMEM((4, rows, feats), BF16),
            pltpu.VMEM((4, 2, heads, rows, HD), BF16),
            pltpu.VMEM((4, 2, heads, rows, HD), BF16),
            pltpu.VMEM((16, rows), F32),
            pltpu.VMEM((2, 16, rows), F32),
            pltpu.VMEM((rows, feats), BF16),
            pltpu.VMEM((2, heads, rows, HD), F32),
            pltpu.VMEM((3, rows, feats), BF16),
            pltpu.VMEM((3, rows, feats), BF16),
            dma((2 + 3 * heads,)),
            dma((3,)),
            dma((3,)),
            dma((2, 2, heads)),
            dma((4, 2, heads)),
            dma((2, 2, heads)),
            dma((4, 2, heads)),
            dma((2,)),
            dma((2,)),
            dma((3,)),
            dma((3,)),
        ],
        compiler_params=pltpu.CompilerParams(
            collective_id=0, has_side_effects=True, vmem_limit_bytes=58 * 1024 * 1024
        ),
    )(queries, key_rows, value_rows, out_weight, cotangent, offs)
    return pl.pallas_call(
        spread,
        out_shape=(tile,) * 4,
        in_specs=[vmem_spec],
        out_specs=(any_spec,) * 4,
        scratch_shapes=[dma((4,))],
    )(four)


def solution(mesh):
    in_specs = (
        P("ctx", "head"),
        P("ctx", "head"),
        P("ctx", "head"),
        P("head", None),
        P("ctx", "head"),
        P(),
    )
    out_specs = (P("ctx", "head"), P("ctx", "head"), P("ctx", "head"), P("ctx", "head"))
    return jax.shard_map(
        functools.partial(per_device, mesh.shape["ctx"]),
        mesh=mesh,
        in_specs=in_specs,
        out_specs=out_specs,
        check_vma=False,
    )
```

```python
import functools
import math

import jax
import jax.numpy as jnp
from jax import lax
from jax.experimental import pallas as pl
from jax.experimental.pallas import tpu as pltpu
from jax.sharding import PartitionSpec as P

HD = 128
BLOCK = 128
PREV = 3
NEG_FILL = -1e30
LOG2E = math.log2(math.e)
F32 = jnp.float32
BF16 = jnp.bfloat16
MESH = pl.DeviceIdType.MESH


def dot_nn(a, b):
    return lax.dot_general(a, b, (((1,), (0,)), ((), ())), preferred_element_type=F32)


def dot_nt(a, b):
    return lax.dot_general(a, b, (((1,), (1,)), ((), ())), preferred_element_type=F32)


def dot_tn(a, b):
    return lax.dot_general(a, b, (((0,), (0,)), ((), ())), preferred_element_type=F32)


def kernel(
    n_ctx, groups, q_hbm, k_hbm, v_hbm, w_hbm, c_hbm, offs,
    out_ref,
    own_q, own_k, own_v, own_do, w_ref, cot, kv, qo, stats, stats_in,
    att, acc, mix_out, mix_in,
    load_sem, cot_send, cot_recv, kv_send, kv_recv, qo_send, qo_recv,
    st_send, st_recv, mix_send, mix_recv, seam_sem,
):
    rows = q_hbm.shape[0]
    feats = q_hbm.shape[1]
    heads = feats // HD
    scale = 1.0 / math.sqrt(HD)
    scale2 = scale * LOG2E
    blocks = rows // BLOCK
    last = blocks - 1
    half = n_ctx // 2
    me = lax.axis_index("ctx")
    grp = lax.axis_index("head")
    first_dev = me == 0
    last_dev = me == n_ctx - 1
    end_dev = me == half - 1
    start_dev = me == half
    at_end = end_dev.astype(jnp.int32)
    at_start = start_dev.astype(jnp.int32)
    is_last = last_dev.astype(jnp.int32)
    is_first = first_dev.astype(jnp.int32)
    key_right = me + 1 + at_end * (n_ctx - 1 - half) + is_last * (half - n_ctx)
    query_left = me - 1 + at_start * (1 - half) + is_first * half
    before_end = me == half - 2
    after_start = me == half + 1
    core = lax.rem(grp, 2)
    pair = grp // 2
    core_mate = pair * 2 + (1 - core)
    x_mate = (1 - pair) * 2 + core
    x_core_mate = (1 - pair) * 2 + (1 - core)

    barrier = pltpu.get_barrier_semaphore()
    def greet(target, sem=barrier):
        pl.semaphore_signal(sem, inc=1, device_id=target, device_id_type=MESH)

    greet((me, core_mate))
    greet((me, x_mate))
    greetings = (
        (me > 0, me - 1),
        ((me < n_ctx - 1) & (me != half - 1), me + 1),
        ((me < n_ctx - 2) & (me != half - 1) & (me != half - 2), me + 2),
        (last_dev, half - 1),
        (start_dev, n_ctx - 1),
        (first_dev, half),
        (first_dev, half - 1),
        (start_dev, half - 2),
        (after_start, half - 1),
    )
    for condition, target in greetings:
        @pl.when(condition)
        def _():
            greet((target, grp))

    def as_int(condition):
        return condition.astype(jnp.int32)

    greeted = (
        2
        + as_int(me < n_ctx - 1)
        + as_int((me > 0) & (me != half))
        + as_int((me > 1) & (me != half) & (me != half + 1))
        + 3 * at_end + is_last + at_start + as_int(before_end)
    )

    def part_rows(b):
        return slice(b * BLOCK, (b + 1) * BLOCK)

    pairs = (
        (c_hbm, cot.at[0]), (w_hbm, w_ref), (q_hbm, own_q), (k_hbm, own_k), (v_hbm, own_v),
    )
    loads = [
        pltpu.make_async_copy(src, dst, load_sem.at[i]) for i, (src, dst) in enumerate(pairs)
    ]
    for copy in loads:
        copy.start()

    def remote(src, dst, send, recv, target):
        return pltpu.make_async_remote_copy(
            src_ref=src, dst_ref=dst, send_sem=send, recv_sem=recv,
            device_id=target, device_id_type=MESH,
        )

    def kv_copy(hop, a, b, src=None):
        slot = hop + 2 * at_end if a == 0 else hop
        return remote(
            kv.at[0, a, part_rows(b)] if src is None else src, kv.at[slot, a, part_rows(b)],
            kv_send.at[hop, a, b], kv_recv.at[slot, a, b],
            (key_right if a == 0 else me + 1, grp),
        )

    def qo_copy(hop, a, b, src=None):
        slot = hop + 2 * at_start if a == 0 else hop
        return remote(
            qo.at[0, a, part_rows(b)] if src is None else src, qo.at[slot, a, part_rows(b)],
            qo_send.at[hop, a, b], qo_recv.at[slot, a, b],
            (query_left if a == 0 else me - 1, grp),
        )

    def arrived(buf, sems, slot, a, b):
        part, sem = buf.at[slot, a, part_rows(b)], sems.at[slot, a, b]
        remote(part, part, sem, sem, (me, core_mate)).wait_recv()

    not_first = jnp.logical_not(first_dev)
    not_last = jnp.logical_not(last_dev)
    inner = (me > 0) & (me < n_ctx - 1)

    def send_own_kv(b):
        @pl.when(not_last)
        def _():
            kv_copy(0, 0, b, k_hbm.at[part_rows(b)]).start()
            kv_copy(0, 1, b, v_hbm.at[part_rows(b)]).start()

    def send_own_qo(a, b):
        @pl.when(not_first)
        def _():
            qo_copy(0, a, b, (q_hbm if a == 0 else own_do).at[part_rows(b)]).start()

    def relay_kv(b):
        for a in range(2):
            @pl.when(not_first)
            def _():
                arrived(kv, kv_recv, 0, a, b)

            @pl.when(inner)
            def _():
                kv_copy(1, a, b).start()

    def wait_far_kv(b):
        for a in range(2):
            @pl.when(me > 1)
            def _():
                arrived(kv, kv_recv, 1, a, b)

    def forward_keys(hop, b):
        @pl.when(last_dev)
        def _():
            arrived(kv, kv_recv, hop + 2, 0, b)
            kv_copy(hop, 0, b, kv.at[hop + 2, 0, part_rows(b)]).start()

    def forward_queries(hop, b):
        @pl.when(first_dev)
        def _():
            arrived(qo, qo_recv, hop + 2, 0, b)
            qo_copy(hop, 0, b, qo.at[hop + 2, 0, part_rows(b)]).start()

    def relay_qo(a, b):
        arrived(qo, qo_recv, 0, a, b)

        @pl.when(me > 0)
        def _():
            qo_copy(1, a, b).start()

    def wait_far_qo(b):
        for a in range(2):
            @pl.when(me < n_ctx - 2)
            def _():
                arrived(qo, qo_recv, 1, a, b)

    def relay_do(b):
        @pl.when(not_last & jnp.logical_not(start_dev))
        def _():
            relay_qo(1, b)

    cot_core = remote(c_hbm, cot.at[1], cot_send.at[0], cot_recv.at[0], (me, core_mate))
    cot_x = remote(c_hbm, cot.at[2], cot_send.at[1], cot_recv.at[1], (me, x_mate))
    cot_relay = remote(cot.at[2], cot.at[3], cot_send.at[2], cot_recv.at[2], (me, core_mate))

    pl.semaphore_wait(barrier, greeted)

    @pl.when(end_dev)
    def _():
        for target in (half, half + 1, 0):
            greet((target, grp), seam_sem)

    @pl.when(before_end)
    def _():
        greet((half, grp), seam_sem)

    cot_x.start()
    cot_core.start()
    order = range(last, -1, -1)
    late_queries = end_dev | before_end
    for b in order:
        @pl.when(jnp.logical_not(end_dev))
        def _():
            send_own_qo(0, b)

        send_own_kv(b)

    @pl.when(first_dev)
    def _():
        kv[0] = jnp.zeros(kv.shape[1:], BF16)

    @pl.when(me <= 1)
    def _():
        kv[1] = jnp.zeros(kv.shape[1:], BF16)

    @pl.when(last_dev)
    def _():
        qo[0] = jnp.zeros(qo.shape[1:], BF16)
        stats_in[0] = jnp.zeros(stats_in.shape[1:], F32)

    @pl.when(me >= n_ctx - 2)
    def _():
        qo[1] = jnp.zeros(qo.shape[1:], BF16)
        stats_in[1] = jnp.zeros(stats_in.shape[1:], F32)

    base = me * rows
    q_pos = base + lax.broadcasted_iota(jnp.int32, (rows, 128), 0)
    first = jnp.zeros((rows, 128), jnp.int32)
    lists = offs[...]
    turned = pltpu.roll(lists, 128 - PREV, 1)
    lane = lax.broadcasted_iota(jnp.int32, lists.shape, 1)
    ahead = jnp.where(lane < 128 - PREV, turned, pltpu.roll(turned, lists.shape[0] - 1, 0))
    for g in range(groups):
        starts = jnp.broadcast_to(lists[g : g + 1, :], (rows, 128))
        later = jnp.broadcast_to(ahead[g : g + 1, :], (rows, 128))
        first = jnp.maximum(first, jnp.where(later <= q_pos, starts, 0))
    first = (first - base).astype(F32)
    low = jnp.max(first.T, axis=0, keepdims=True)
    stats[...] = jnp.zeros(stats.shape, F32)
    for b in order:
        stats[b, 2 * heads : 2 * heads + 1, :] = low[:, part_rows(b)]

    def w_block(index):
        return w_ref[:, pl.ds(pl.multiple_of(index * feats, feats), feats)]

    loads[0].wait()
    loads[1].wait()
    grad = dot_nt(cot[0], w_block(grp))
    cot_core.wait_recv()
    grad += dot_nt(cot[1], w_block(core_mate))

    @pl.when(not_last & jnp.logical_not(late_queries))
    def _():
        for b in order:
            relay_qo(0, b)

    @pl.when(jnp.logical_not(start_dev))
    def _():
        relay_kv(last)

    cot_x.wait_recv()
    cot_relay.start()
    grad += dot_nt(cot[2], w_block(x_mate))
    for b in order[:-1]:
        forward_keys(0, b)

    @pl.when(jnp.logical_not(start_dev))
    def _():
        for b in order[1:-1]:
            relay_kv(b)

    @pl.when(end_dev)
    def _():
        for b in order:
            send_own_qo(0, b)

    cot_relay.wait_recv()
    grad += dot_nt(cot[3], w_block(x_core_mate))
    own_do[...] = grad.astype(BF16)

    @pl.when(start_dev)
    def _():
        pl.semaphore_wait(seam_sem, 2)

    @pl.when(first_dev)
    def _():
        pl.semaphore_wait(seam_sem, 1)

    @pl.when(after_start)
    def _():
        pl.semaphore_wait(seam_sem, 1)

    for b in order:
        send_own_qo(1, b)

    @pl.when(start_dev)
    def _():
        for b in order:
            relay_qo(1, b)

    for b in order:
        forward_queries(0, b)
    for copy in loads[2:]:
        copy.wait()

    def head_cols(h):
        return slice(h * HD, (h + 1) * HD)

    def query_side(b):
        part = part_rows(b)
        floor = low[:, part]
        for h in range(heads):
            col = head_cols(h)
            query = own_q[part, col]
            grad_o = own_do[part, col]
            own_rows = slice(0, (b + 1) * BLOCK)
            far_rows = slice(b * BLOCK, rows)
            key_tiles = (own_k[own_rows, col], kv[0, 0, :, col], kv[1, 0, far_rows, col])
            value_tiles = (own_v[own_rows, col], kv[0, 1, :, col], kv[1, 1, far_rows, col])
            scores = []
            for d in range(3):
                shape = (key_tiles[d].shape[0], BLOCK)
                start = b * BLOCK if d == 2 else 0
                key_row = lax.broadcasted_iota(jnp.int32, shape, 0).astype(F32)
                mask = key_row >= floor + float(d * rows - start)
                if d == 0:
                    query_col = lax.broadcasted_iota(jnp.int32, shape, 1).astype(F32)
                    mask = mask & (key_row <= query_col + float(b * BLOCK))
                raw = dot_nt(key_tiles[d], query) * scale2
                scores.append(jnp.where(mask, raw, NEG_FILL))
            top = functools.reduce(
                jnp.maximum, [jnp.max(s, axis=0, keepdims=True) for s in scores]
            )
            expd = [jnp.exp2(s - top) for s in scores]
            total = functools.reduce(jnp.add, [jnp.sum(e, axis=0, keepdims=True) for e in expd])
            inverse = 1.0 / total
            probs = [e * inverse for e in expd]
            probs_b = [p.astype(BF16) for p in probs]
            mixed_t = sum(dot_tn(value_tiles[d], probs_b[d]) for d in range(3))
            attended = mixed_t.T.astype(BF16)
            att[part, col] = attended
            product = grad_o.astype(F32) * attended.astype(F32)
            delta = jnp.sum(product.T, axis=0, keepdims=True)
            stats[b, h : h + 1, :] = top + jnp.log2(total)
            stats[b, heads + h : heads + h + 1, :] = delta
            grads_b = []
            for d in range(3):
                grad_p = dot_nt(value_tiles[d], grad_o)
                grads_b.append((scale * probs[d] * (grad_p - delta)).astype(BF16))
            dq_t = sum(dot_tn(key_tiles[d], grads_b[d]) for d in range(3))
            out_ref[1, part, col] = dq_t.T.astype(BF16)
            grad_k = dot_nn(grads_b[0], query)
            grad_v = dot_nn(probs_b[0], grad_o)
            if b == last:
                acc[0, :, col] = grad_k
                acc[1, :, col] = grad_v
            else:
                acc[0, own_rows, col] += grad_k
                acc[1, own_rows, col] += grad_v

    def key_side(b):
        part = part_rows(b)
        for h in range(heads):
            col = head_cols(h)
            for d in range(2):
                start = b * BLOCK if d == 1 else 0
                near = slice(start, rows)
                query = qo[d, 0, part, col]
                grad_o = qo[d, 1, part, col]
                key_row = lax.broadcasted_iota(jnp.int32, (rows - start, BLOCK), 0).astype(F32)
                floor = stats_in[d, b, 2 * heads : 2 * heads + 1, :]
                floor = floor + float((d + 1) * rows - start)
                log_total = stats_in[d, b, h : h + 1, :]
                delta = stats_in[d, b, heads + h : heads + h + 1, :]
                raw = dot_nt(own_k[near, col], query) * scale2
                probs = jnp.where(key_row >= floor, jnp.exp2(raw - log_total), 0.0)
                acc[1, near, col] += dot_nn(probs.astype(BF16), grad_o)
                grad_p = dot_nt(own_v[near, col], grad_o)
                grad_s = (scale * probs * (grad_p - delta)).astype(BF16)
                acc[0, near, col] += dot_nn(grad_s, query)

    def stat_copy(b, d):
        return remote(
            stats.at[b], stats_in.at[d, b], st_send.at[d, b], st_recv.at[d, b], (me - 1 - d, grp)
        )

    def send_stats(b):
        for d in range(2):
            @pl.when(me > d)
            def _():
                stat_copy(b, d).start()

    def wait_queries(b):
        wait_far_qo(b)
        for d in range(2):
            @pl.when(me < n_ctx - 1 - d)
            def _():
                stat_copy(b, d).wait_recv()

    def mix_copy(i, b):
        part = part_rows(b)
        return remote(
            mix_out.at[i, part], mix_in.at[i, part], mix_send.at[i, b], mix_recv.at[i, b],
            (me, x_mate if i == 2 else core_mate),
        )

    def mix_near(b):
        part = part_rows(b)
        for i, owner in enumerate((x_core_mate, core_mate)):
            mix_out[i, part] = dot_nn(att[part], w_block(owner)).astype(BF16)
            mix_copy(i, b).start()

    def mix_far(b):
        part = part_rows(b)
        far_part = dot_nn(att[part], w_block(x_mate))
        mix_copy(0, b).wait_recv()
        mix_out[2, part] = (far_part + mix_in[0, part].astype(F32)).astype(BF16)
        mix_copy(2, b).start()

    def mix_finish(b):
        part = part_rows(b)
        own_part = dot_nn(att[part], w_block(grp))
        mix_copy(1, b).wait_recv()
        own_part += mix_in[1, part].astype(F32)
        mix_copy(2, b).wait_recv()
        out_ref[0, part] = (own_part + mix_in[2, part].astype(F32)).astype(BF16)

    @pl.when(start_dev)
    def _():
        for b in order[:-1]:
            relay_kv(b)

    for b in order:
        forward_queries(1, b)
    relay_kv(0)
    forward_keys(0, 0)

    @pl.when(late_queries)
    def _():
        for b in order:
            relay_qo(0, b)

    for b in order[:-1]:
        forward_keys(1, b)
    relay_do(last)
    for b in order:
        wait_far_kv(b)
        if b == last:
            forward_keys(1, 0)
        query_side(b)
        send_stats(b)
        mix_near(b)
        if b == last:
            for later in order[1:]:
                relay_do(later)
        elif b > 0:
            wait_queries(b + 1)
            key_side(b + 1)
        mix_far(b)
    wait_queries(1)
    key_side(1)
    wait_queries(0)
    key_side(0)
    out_ref[2] = acc[0].astype(BF16)
    out_ref[3] = acc[1].astype(BF16)
    for b in order:
        mix_finish(b)

    cot_core.wait_send()
    cot_x.wait_send()
    cot_relay.wait_send()
    for b in order:
        kv_copy(0, 0, b).wait_send()
        qo_copy(0, 0, b).wait_send()

        @pl.when(not_last)
        def _():
            kv_copy(0, 1, b).wait_send()
            qo_copy(1, 0, b).wait_send()

        @pl.when(not_first)
        def _():
            qo_copy(0, 1, b).wait_send()
            kv_copy(1, 0, b).wait_send()

        @pl.when(inner)
        def _():
            kv_copy(1, 1, b).wait_send()
            qo_copy(1, 1, b).wait_send()

    for b in order:
        for d in range(2):
            @pl.when(me > d)
            def _():
                stat_copy(b, d).wait_send()
        for i in range(3):
            mix_copy(i, b).wait_send()


def spread(all_ref, *refs):
    outs, sems = refs[:-1], refs[-1]
    copies = [
        pltpu.make_async_copy(all_ref.at[i], out, sems.at[i]) for i, out in enumerate(outs)
    ]
    for copy in copies:
        copy.start()
    for copy in copies:
        copy.wait()


def per_device(n_ctx, queries, key_rows, value_rows, out_weight, cotangent, offsets):
    rows, feats = queries.shape
    blocks = rows // BLOCK
    count = offsets.shape[0]
    groups = -(-count // 128)
    padded = -(-(groups + 1) // 8) * 8
    offs = jnp.pad(offsets, (0, padded * 128 - count), constant_values=2**30)
    offs = offs.reshape(padded, 128)
    any_spec = pl.BlockSpec(memory_space=pl.ANY)
    vmem_spec = pl.BlockSpec(memory_space=pltpu.VMEM)
    tile = jax.ShapeDtypeStruct((rows, feats), BF16)
    dma = pltpu.SemaphoreType.DMA
    four = pl.pallas_call(
        functools.partial(kernel, n_ctx, groups),
        out_shape=jax.ShapeDtypeStruct((4, rows, feats), BF16),
        in_specs=[any_spec] * 5 + [vmem_spec],
        out_specs=vmem_spec,
        scratch_shapes=[
            pltpu.VMEM((rows, feats), BF16),
            pltpu.VMEM((rows, feats), BF16),
            pltpu.VMEM((rows, feats), BF16),
            pltpu.VMEM((rows, feats), BF16),
            pltpu.VMEM(out_weight.shape, BF16),
            pltpu.VMEM((4, rows, feats), BF16),
            pltpu.VMEM((4, 2, rows, feats), BF16),
            pltpu.VMEM((4, 2, rows, feats), BF16),
            pltpu.VMEM((blocks, 16, BLOCK), F32),
            pltpu.VMEM((2, blocks, 16, BLOCK), F32),
            pltpu.VMEM((rows, feats), BF16),
            pltpu.VMEM((2, rows, feats), F32),
            pltpu.VMEM((3, rows, feats), BF16),
            pltpu.VMEM((3, rows, feats), BF16),
            dma((5,)),
            dma((3,)),
            dma((3,)),
            dma((2, 2, blocks)),
            dma((4, 2, blocks)),
            dma((2, 2, blocks)),
            dma((4, 2, blocks)),
            dma((2, blocks)),
            dma((2, blocks)),
            dma((3, blocks)),
            dma((3, blocks)),
            pltpu.SemaphoreType.REGULAR,
        ],
        compiler_params=pltpu.CompilerParams(
            collective_id=0, has_side_effects=True, vmem_limit_bytes=58 * 1024 * 1024
        ),
    )(queries, key_rows, value_rows, out_weight, cotangent, offs)
    return pl.pallas_call(
        spread,
        out_shape=(tile,) * 4,
        in_specs=[vmem_spec],
        out_specs=(any_spec,) * 4,
        scratch_shapes=[dma((4,))],
    )(four)


def solution(mesh):
    in_specs = (
        P("ctx", "head"),
        P("ctx", "head"),
        P("ctx", "head"),
        P("head", None),
        P("ctx", "head"),
        P(),
    )
    out_specs = (P("ctx", "head"), P("ctx", "head"), P("ctx", "head"), P("ctx", "head"))
    return jax.shard_map(
        functools.partial(per_device, mesh.shape["ctx"]),
        mesh=mesh,
        in_specs=in_specs,
        out_specs=out_specs,
        check_vma=False,
    )
```

```python
import functools
import math

import jax
import jax.numpy as jnp
from jax import lax
from jax.experimental import pallas as pl
from jax.experimental.pallas import tpu as pltpu
from jax.sharding import PartitionSpec as P

HD = 128
BLOCK = 128
PREV = 3
NEG_FILL = -1e30
LOG2E = math.log2(math.e)
F32 = jnp.float32
BF16 = jnp.bfloat16
MESH = pl.DeviceIdType.MESH


def dot_nn(a, b):
    return lax.dot_general(a, b, (((1,), (0,)), ((), ())), preferred_element_type=F32)


def dot_nt(a, b):
    return lax.dot_general(a, b, (((1,), (1,)), ((), ())), preferred_element_type=F32)


def dot_tn(a, b):
    return lax.dot_general(a, b, (((0,), (0,)), ((), ())), preferred_element_type=F32)


def kernel(
    n_ctx, groups, q_hbm, k_hbm, v_hbm, w_hbm, c_hbm, offs,
    out_ref,
    own_q, own_k, own_v, own_do, w_ref, cot, kv, qo, stats, stats_in,
    att, acc, mix_out, mix_in,
    load_sem, cot_send, cot_recv, kv_send, kv_recv, qo_send, qo_recv,
    st_send, st_recv, mix_send, mix_recv, seam_sem,
):
    rows = q_hbm.shape[0]
    feats = q_hbm.shape[1]
    heads = feats // HD
    scale = 1.0 / math.sqrt(HD)
    scale2 = scale * LOG2E
    blocks = rows // BLOCK
    last = blocks - 1
    half = n_ctx // 2
    me = lax.axis_index("ctx")
    grp = lax.axis_index("head")
    first_dev = me == 0
    last_dev = me == n_ctx - 1
    end_dev = me == half - 1
    start_dev = me == half
    at_end = end_dev.astype(jnp.int32)
    at_start = start_dev.astype(jnp.int32)
    is_last = last_dev.astype(jnp.int32)
    is_first = first_dev.astype(jnp.int32)
    key_right = me + 1 + at_end * (n_ctx - 1 - half) + is_last * (half - n_ctx)
    query_left = me - 1 + at_start * (1 - half) + is_first * half
    before_end = me == half - 2
    after_start = me == half + 1
    core = lax.rem(grp, 2)
    pair = grp // 2
    core_mate = pair * 2 + (1 - core)
    x_mate = (1 - pair) * 2 + core
    x_core_mate = (1 - pair) * 2 + (1 - core)

    barrier = pltpu.get_barrier_semaphore()
    def greet(target, sem=barrier):
        pl.semaphore_signal(sem, inc=1, device_id=target, device_id_type=MESH)

    greet((me, core_mate))
    greet((me, x_mate))
    greetings = (
        (me > 0, me - 1),
        ((me < n_ctx - 1) & (me != half - 1), me + 1),
        ((me < n_ctx - 2) & (me != half - 1) & (me != half - 2), me + 2),
        (last_dev, half - 1),
        (start_dev, n_ctx - 1),
        (first_dev, half),
        (first_dev, half - 1),
        (start_dev, half - 2),
        (after_start, half - 1),
    )
    for condition, target in greetings:
        @pl.when(condition)
        def _():
            greet((target, grp))

    def as_int(condition):
        return condition.astype(jnp.int32)

    greeted = (
        2
        + as_int(me < n_ctx - 1)
        + as_int((me > 0) & (me != half))
        + as_int((me > 1) & (me != half) & (me != half + 1))
        + 3 * at_end + is_last + at_start + as_int(before_end)
    )

    def part_rows(b):
        return slice(b * BLOCK, (b + 1) * BLOCK)

    pairs = (
        (c_hbm, cot.at[0]), (w_hbm, w_ref), (q_hbm, own_q), (k_hbm, own_k), (v_hbm, own_v),
    )
    loads = [
        pltpu.make_async_copy(src, dst, load_sem.at[i]) for i, (src, dst) in enumerate(pairs)
    ]
    for copy in loads:
        copy.start()

    def remote(src, dst, send, recv, target):
        return pltpu.make_async_remote_copy(
            src_ref=src, dst_ref=dst, send_sem=send, recv_sem=recv,
            device_id=target, device_id_type=MESH,
        )

    def kv_copy(hop, a, b, src=None):
        slot = hop + 2 * at_end if a == 0 else hop
        return remote(
            kv.at[0, a, part_rows(b)] if src is None else src, kv.at[slot, a, part_rows(b)],
            kv_send.at[hop, a, b], kv_recv.at[slot, a, b],
            (key_right if a == 0 else me + 1, grp),
        )

    def qo_copy(hop, a, b, src=None):
        slot = hop + 2 * at_start if a == 0 else hop
        return remote(
            qo.at[0, a, part_rows(b)] if src is None else src, qo.at[slot, a, part_rows(b)],
            qo_send.at[hop, a, b], qo_recv.at[slot, a, b],
            (query_left if a == 0 else me - 1, grp),
        )

    def arrived(buf, sems, slot, a, b):
        part, sem = buf.at[slot, a, part_rows(b)], sems.at[slot, a, b]
        remote(part, part, sem, sem, (me, core_mate)).wait_recv()

    not_first = jnp.logical_not(first_dev)
    not_last = jnp.logical_not(last_dev)
    inner = (me > 0) & (me < n_ctx - 1)

    def send_own_kv(b):
        @pl.when(not_last)
        def _():
            kv_copy(0, 0, b, k_hbm.at[part_rows(b)]).start()
            kv_copy(0, 1, b, v_hbm.at[part_rows(b)]).start()

    def send_own_qo(a, b):
        @pl.when(not_first)
        def _():
            qo_copy(0, a, b, (q_hbm if a == 0 else own_do).at[part_rows(b)]).start()

    def relay_kv(b):
        for a in range(2):
            @pl.when(not_first)
            def _():
                arrived(kv, kv_recv, 0, a, b)

            @pl.when(inner)
            def _():
                kv_copy(1, a, b).start()

    def wait_far_kv(b):
        for a in range(2):
            @pl.when(me > 1)
            def _():
                arrived(kv, kv_recv, 1, a, b)

    def forward_keys(hop, b):
        @pl.when(last_dev)
        def _():
            arrived(kv, kv_recv, hop + 2, 0, b)
            kv_copy(hop, 0, b, kv.at[hop + 2, 0, part_rows(b)]).start()

    def forward_queries(hop, b):
        @pl.when(first_dev)
        def _():
            arrived(qo, qo_recv, hop + 2, 0, b)
            qo_copy(hop, 0, b, qo.at[hop + 2, 0, part_rows(b)]).start()

    def relay_qo(a, b):
        arrived(qo, qo_recv, 0, a, b)

        @pl.when(me > 0)
        def _():
            qo_copy(1, a, b).start()

    def wait_far_qo(b):
        for a in range(2):
            @pl.when(me < n_ctx - 2)
            def _():
                arrived(qo, qo_recv, 1, a, b)

    def relay_do(b):
        @pl.when(not_last & jnp.logical_not(start_dev))
        def _():
            relay_qo(1, b)

    cot_core = remote(c_hbm, cot.at[1], cot_send.at[0], cot_recv.at[0], (me, core_mate))
    cot_x = remote(c_hbm, cot.at[2], cot_send.at[1], cot_recv.at[1], (me, x_mate))
    cot_relay = remote(cot.at[2], cot.at[3], cot_send.at[2], cot_recv.at[2], (me, core_mate))

    pl.semaphore_wait(barrier, greeted)

    @pl.when(end_dev)
    def _():
        for target in (half, half + 1, 0):
            greet((target, grp), seam_sem)

    @pl.when(before_end)
    def _():
        greet((half, grp), seam_sem)

    cot_x.start()
    cot_core.start()
    order = range(last, -1, -1)
    late_queries = end_dev | before_end
    for b in order:
        @pl.when(jnp.logical_not(end_dev))
        def _():
            send_own_qo(0, b)

        send_own_kv(b)

    @pl.when(first_dev)
    def _():
        kv[0] = jnp.zeros(kv.shape[1:], BF16)

    @pl.when(me <= 1)
    def _():
        kv[1] = jnp.zeros(kv.shape[1:], BF16)

    @pl.when(last_dev)
    def _():
        qo[0] = jnp.zeros(qo.shape[1:], BF16)
        stats_in[0] = jnp.zeros(stats_in.shape[1:], F32)

    @pl.when(me >= n_ctx - 2)
    def _():
        qo[1] = jnp.zeros(qo.shape[1:], BF16)
        stats_in[1] = jnp.zeros(stats_in.shape[1:], F32)

    base = me * rows
    q_pos = base + lax.broadcasted_iota(jnp.int32, (rows, 128), 0)
    first = jnp.zeros((rows, 128), jnp.int32)
    lists = offs[...]
    turned = pltpu.roll(lists, 128 - PREV, 1)
    lane = lax.broadcasted_iota(jnp.int32, lists.shape, 1)
    ahead = jnp.where(lane < 128 - PREV, turned, pltpu.roll(turned, lists.shape[0] - 1, 0))
    for g in range(groups):
        starts = jnp.broadcast_to(lists[g : g + 1, :], (rows, 128))
        later = jnp.broadcast_to(ahead[g : g + 1, :], (rows, 128))
        first = jnp.maximum(first, jnp.where(later <= q_pos, starts, 0))
    first = (first - base).astype(F32)
    low = jnp.max(first.T, axis=0, keepdims=True)
    stats[...] = jnp.zeros(stats.shape, F32)
    for b in order:
        stats[b, 2 * heads : 2 * heads + 1, :] = low[:, part_rows(b)]

    def w_block(index):
        return w_ref[:, pl.ds(pl.multiple_of(index * feats, feats), feats)]

    loads[0].wait()
    loads[1].wait()
    grad = dot_nt(cot[0], w_block(grp))
    cot_core.wait_recv()
    grad += dot_nt(cot[1], w_block(core_mate))

    @pl.when(not_last & jnp.logical_not(late_queries))
    def _():
        for b in order:
            relay_qo(0, b)

    @pl.when(jnp.logical_not(start_dev))
    def _():
        relay_kv(last)

    cot_x.wait_recv()
    cot_relay.start()
    grad += dot_nt(cot[2], w_block(x_mate))
    for b in order[:-1]:
        forward_keys(0, b)

    @pl.when(jnp.logical_not(start_dev))
    def _():
        for b in order[1:-1]:
            relay_kv(b)

    cot_relay.wait_recv()
    grad += dot_nt(cot[3], w_block(x_core_mate))
    own_do[...] = grad.astype(BF16)

    @pl.when(start_dev)
    def _():
        pl.semaphore_wait(seam_sem, 2)

    @pl.when(first_dev)
    def _():
        pl.semaphore_wait(seam_sem, 1)

    @pl.when(after_start)
    def _():
        pl.semaphore_wait(seam_sem, 1)

    @pl.when(end_dev)
    def _():
        relay_kv(0)

    for b in order:
        send_own_qo(1, b)

    @pl.when(end_dev)
    def _():
        for b in order:
            send_own_qo(0, b)

    @pl.when(start_dev)
    def _():
        for b in order:
            relay_kv(b)
            relay_qo(1, b)

    for b in order:
        forward_queries(0, b)
    for copy in loads[2:]:
        copy.wait()

    def head_cols(h):
        return slice(h * HD, (h + 1) * HD)

    def query_side(b):
        part = part_rows(b)
        floor = low[:, part]
        for h in range(heads):
            col = head_cols(h)
            query = own_q[part, col]
            grad_o = own_do[part, col]
            own_rows = slice(0, (b + 1) * BLOCK)
            far_rows = slice(b * BLOCK, rows)
            key_tiles = (own_k[own_rows, col], kv[0, 0, :, col], kv[1, 0, far_rows, col])
            value_tiles = (own_v[own_rows, col], kv[0, 1, :, col], kv[1, 1, far_rows, col])
            scores = []
            for d in range(3):
                shape = (key_tiles[d].shape[0], BLOCK)
                start = b * BLOCK if d == 2 else 0
                key_row = lax.broadcasted_iota(jnp.int32, shape, 0).astype(F32)
                mask = key_row >= floor + float(d * rows - start)
                if d == 0:
                    query_col = lax.broadcasted_iota(jnp.int32, shape, 1).astype(F32)
                    mask = mask & (key_row <= query_col + float(b * BLOCK))
                raw = dot_nt(key_tiles[d], query) * scale2
                scores.append(jnp.where(mask, raw, NEG_FILL))
            top = functools.reduce(
                jnp.maximum, [jnp.max(s, axis=0, keepdims=True) for s in scores]
            )
            expd = [jnp.exp2(s - top) for s in scores]
            total = functools.reduce(jnp.add, [jnp.sum(e, axis=0, keepdims=True) for e in expd])
            inverse = 1.0 / total
            probs = [e * inverse for e in expd]
            probs_b = [p.astype(BF16) for p in probs]
            mixed_t = sum(dot_tn(value_tiles[d], probs_b[d]) for d in range(3))
            attended = mixed_t.T.astype(BF16)
            att[part, col] = attended
            product = grad_o.astype(F32) * attended.astype(F32)
            delta = jnp.sum(product.T, axis=0, keepdims=True)
            stats[b, h : h + 1, :] = top + jnp.log2(total)
            stats[b, heads + h : heads + h + 1, :] = delta
            grads_b = []
            for d in range(3):
                grad_p = dot_nt(value_tiles[d], grad_o)
                grads_b.append((scale * probs[d] * (grad_p - delta)).astype(BF16))
            dq_t = sum(dot_tn(key_tiles[d], grads_b[d]) for d in range(3))
            out_ref[1, part, col] = dq_t.T.astype(BF16)
            grad_k = dot_nn(grads_b[0], query)
            grad_v = dot_nn(probs_b[0], grad_o)
            if b == last:
                acc[0, :, col] = grad_k
                acc[1, :, col] = grad_v
            else:
                acc[0, own_rows, col] += grad_k
                acc[1, own_rows, col] += grad_v

    def key_side(b):
        part = part_rows(b)
        for h in range(heads):
            col = head_cols(h)
            for d in range(2):
                start = b * BLOCK if d == 1 else 0
                near = slice(start, rows)
                query = qo[d, 0, part, col]
                grad_o = qo[d, 1, part, col]
                key_row = lax.broadcasted_iota(jnp.int32, (rows - start, BLOCK), 0).astype(F32)
                floor = stats_in[d, b, 2 * heads : 2 * heads + 1, :]
                floor = floor + float((d + 1) * rows - start)
                log_total = stats_in[d, b, h : h + 1, :]
                delta = stats_in[d, b, heads + h : heads + h + 1, :]
                raw = dot_nt(own_k[near, col], query) * scale2
                probs = jnp.where(key_row >= floor, jnp.exp2(raw - log_total), 0.0)
                acc[1, near, col] += dot_nn(probs.astype(BF16), grad_o)
                grad_p = dot_nt(own_v[near, col], grad_o)
                grad_s = (scale * probs * (grad_p - delta)).astype(BF16)
                acc[0, near, col] += dot_nn(grad_s, query)

    def stat_copy(b, d):
        return remote(
            stats.at[b], stats_in.at[d, b], st_send.at[d, b], st_recv.at[d, b], (me - 1 - d, grp)
        )

    def send_stats(b):
        for d in range(2):
            @pl.when(me > d)
            def _():
                stat_copy(b, d).start()

    def wait_queries(b):
        wait_far_qo(b)
        for d in range(2):
            @pl.when(me < n_ctx - 1 - d)
            def _():
                stat_copy(b, d).wait_recv()

    def mix_copy(i, b):
        part = part_rows(b)
        return remote(
            mix_out.at[i, part], mix_in.at[i, part], mix_send.at[i, b], mix_recv.at[i, b],
            (me, x_mate if i == 2 else core_mate),
        )

    def mix_near(b):
        part = part_rows(b)
        for i, owner in enumerate((x_core_mate, core_mate)):
            mix_out[i, part] = dot_nn(att[part], w_block(owner)).astype(BF16)
            mix_copy(i, b).start()

    def mix_far(b):
        part = part_rows(b)
        far_part = dot_nn(att[part], w_block(x_mate))
        mix_copy(0, b).wait_recv()
        mix_out[2, part] = (far_part + mix_in[0, part].astype(F32)).astype(BF16)
        mix_copy(2, b).start()

    def mix_finish(b):
        part = part_rows(b)
        own_part = dot_nn(att[part], w_block(grp))
        mix_copy(1, b).wait_recv()
        own_part += mix_in[1, part].astype(F32)
        mix_copy(2, b).wait_recv()
        out_ref[0, part] = (own_part + mix_in[2, part].astype(F32)).astype(BF16)

    for b in order:
        forward_queries(1, b)

    @pl.when(jnp.logical_not(end_dev | start_dev))
    def _():
        relay_kv(0)

    forward_keys(0, 0)
    for b in order[:-1]:
        forward_keys(1, b)
    relay_do(last)
    for b in order:
        wait_far_kv(b)
        if b == last:
            forward_keys(1, 0)
        query_side(b)
        send_stats(b)
        mix_near(b)
        if b == last:
            @pl.when(late_queries)
            def _():
                for late in order:
                    relay_qo(0, late)

            for later in order[1:]:
                relay_do(later)
        elif b > 0:
            wait_queries(b + 1)
            key_side(b + 1)
        mix_far(b)
    wait_queries(1)
    key_side(1)
    wait_queries(0)
    key_side(0)
    out_ref[2] = acc[0].astype(BF16)
    out_ref[3] = acc[1].astype(BF16)
    for b in order:
        mix_finish(b)

    cot_core.wait_send()
    cot_x.wait_send()
    cot_relay.wait_send()
    for b in order:
        kv_copy(0, 0, b).wait_send()
        qo_copy(0, 0, b).wait_send()

        @pl.when(not_last)
        def _():
            kv_copy(0, 1, b).wait_send()
            qo_copy(1, 0, b).wait_send()

        @pl.when(not_first)
        def _():
            qo_copy(0, 1, b).wait_send()
            kv_copy(1, 0, b).wait_send()

        @pl.when(inner)
        def _():
            kv_copy(1, 1, b).wait_send()
            qo_copy(1, 1, b).wait_send()

    for b in order:
        for d in range(2):
            @pl.when(me > d)
            def _():
                stat_copy(b, d).wait_send()
        for i in range(3):
            mix_copy(i, b).wait_send()


def spread(all_ref, *refs):
    outs, sems = refs[:-1], refs[-1]
    copies = [
        pltpu.make_async_copy(all_ref.at[i], out, sems.at[i]) for i, out in enumerate(outs)
    ]
    for copy in copies:
        copy.start()
    for copy in copies:
        copy.wait()


def per_device(n_ctx, queries, key_rows, value_rows, out_weight, cotangent, offsets):
    rows, feats = queries.shape
    blocks = rows // BLOCK
    count = offsets.shape[0]
    groups = -(-count // 128)
    padded = -(-(groups + 1) // 8) * 8
    offs = jnp.pad(offsets, (0, padded * 128 - count), constant_values=2**30)
    offs = offs.reshape(padded, 128)
    any_spec = pl.BlockSpec(memory_space=pl.ANY)
    vmem_spec = pl.BlockSpec(memory_space=pltpu.VMEM)
    tile = jax.ShapeDtypeStruct((rows, feats), BF16)
    dma = pltpu.SemaphoreType.DMA
    four = pl.pallas_call(
        functools.partial(kernel, n_ctx, groups),
        out_shape=jax.ShapeDtypeStruct((4, rows, feats), BF16),
        in_specs=[any_spec] * 5 + [vmem_spec],
        out_specs=vmem_spec,
        scratch_shapes=[
            pltpu.VMEM((rows, feats), BF16),
            pltpu.VMEM((rows, feats), BF16),
            pltpu.VMEM((rows, feats), BF16),
            pltpu.VMEM((rows, feats), BF16),
            pltpu.VMEM(out_weight.shape, BF16),
            pltpu.VMEM((4, rows, feats), BF16),
            pltpu.VMEM((4, 2, rows, feats), BF16),
            pltpu.VMEM((4, 2, rows, feats), BF16),
            pltpu.VMEM((blocks, 16, BLOCK), F32),
            pltpu.VMEM((2, blocks, 16, BLOCK), F32),
            pltpu.VMEM((rows, feats), BF16),
            pltpu.VMEM((2, rows, feats), F32),
            pltpu.VMEM((3, rows, feats), BF16),
            pltpu.VMEM((3, rows, feats), BF16),
            dma((5,)),
            dma((3,)),
            dma((3,)),
            dma((2, 2, blocks)),
            dma((4, 2, blocks)),
            dma((2, 2, blocks)),
            dma((4, 2, blocks)),
            dma((2, blocks)),
            dma((2, blocks)),
            dma((3, blocks)),
            dma((3, blocks)),
            pltpu.SemaphoreType.REGULAR,
        ],
        compiler_params=pltpu.CompilerParams(
            collective_id=0, has_side_effects=True, vmem_limit_bytes=58 * 1024 * 1024
        ),
    )(queries, key_rows, value_rows, out_weight, cotangent, offs)
    return pl.pallas_call(
        spread,
        out_shape=(tile,) * 4,
        in_specs=[vmem_spec],
        out_specs=(any_spec,) * 4,
        scratch_shapes=[dma((4,))],
    )(four)


def solution(mesh):
    in_specs = (
        P("ctx", "head"),
        P("ctx", "head"),
        P("ctx", "head"),
        P("head", None),
        P("ctx", "head"),
        P(),
    )
    out_specs = (P("ctx", "head"), P("ctx", "head"), P("ctx", "head"), P("ctx", "head"))
    return jax.shard_map(
        functools.partial(per_device, mesh.shape["ctx"]),
        mesh=mesh,
        in_specs=in_specs,
        out_specs=out_specs,
        check_vma=False,
    )
```

```python
import functools
import math

import jax
import jax.numpy as jnp
from jax import lax
from jax.experimental import pallas as pl
from jax.experimental.pallas import tpu as pltpu
from jax.sharding import PartitionSpec as P

HD = 128
BLOCK = 128
PREV = 3
NEG_FILL = -1e30
LOG2E = math.log2(math.e)
F32 = jnp.float32
BF16 = jnp.bfloat16
MESH = pl.DeviceIdType.MESH


def dot_nn(a, b):
    return lax.dot_general(a, b, (((1,), (0,)), ((), ())), preferred_element_type=F32)


def dot_nt(a, b):
    return lax.dot_general(a, b, (((1,), (1,)), ((), ())), preferred_element_type=F32)


def dot_tn(a, b):
    return lax.dot_general(a, b, (((0,), (0,)), ((), ())), preferred_element_type=F32)


def kernel(
    n_ctx, groups, q_hbm, k_hbm, v_hbm, w_hbm, c_hbm, offs,
    out_ref,
    own_q, own_k, own_v, own_do, w_ref, cot, kv, qo, stats, stats_in,
    att, acc, mix_out, mix_in,
    load_sem, cot_send, cot_recv, kv_send, kv_recv, qo_send, qo_recv,
    st_send, st_recv, mix_send, mix_recv, seam_sem,
):
    rows = q_hbm.shape[0]
    feats = q_hbm.shape[1]
    heads = feats // HD
    scale = 1.0 / math.sqrt(HD)
    scale2 = scale * LOG2E
    blocks = rows // BLOCK
    last = blocks - 1
    half = n_ctx // 2
    me = lax.axis_index("ctx")
    grp = lax.axis_index("head")
    first_dev = me == 0
    last_dev = me == n_ctx - 1
    end_dev = me == half - 1
    start_dev = me == half
    at_end = end_dev.astype(jnp.int32)
    at_start = start_dev.astype(jnp.int32)
    is_last = last_dev.astype(jnp.int32)
    is_first = first_dev.astype(jnp.int32)
    key_right = me + 1 + at_end * (n_ctx - 1 - half) + is_last * (half - n_ctx)
    query_left = me - 1 + at_start * (1 - half) + is_first * half
    before_end = me == half - 2
    after_start = me == half + 1
    core = lax.rem(grp, 2)
    pair = grp // 2
    core_mate = pair * 2 + (1 - core)
    x_mate = (1 - pair) * 2 + core
    x_core_mate = (1 - pair) * 2 + (1 - core)

    barrier = pltpu.get_barrier_semaphore()
    def greet(target, sem=barrier):
        pl.semaphore_signal(sem, inc=1, device_id=target, device_id_type=MESH)

    greet((me, core_mate))
    greet((me, x_mate))
    greetings = (
        (me > 0, me - 1),
        ((me < n_ctx - 1) & (me != half - 1), me + 1),
        ((me < n_ctx - 2) & (me != half - 1) & (me != half - 2), me + 2),
        (last_dev, half - 1),
        (start_dev, n_ctx - 1),
        (first_dev, half),
        (first_dev, half - 1),
        (start_dev, half - 2),
        (after_start, half - 1),
    )
    for condition, target in greetings:
        @pl.when(condition)
        def _():
            greet((target, grp))

    def as_int(condition):
        return condition.astype(jnp.int32)

    greeted = (
        2
        + as_int(me < n_ctx - 1)
        + as_int((me > 0) & (me != half))
        + as_int((me > 1) & (me != half) & (me != half + 1))
        + 3 * at_end + is_last + at_start + as_int(before_end)
    )

    def part_rows(b):
        return slice(b * BLOCK, (b + 1) * BLOCK)

    pairs = (
        (c_hbm, cot.at[0]), (w_hbm, w_ref), (q_hbm, own_q), (k_hbm, own_k), (v_hbm, own_v),
    )
    loads = [
        pltpu.make_async_copy(src, dst, load_sem.at[i]) for i, (src, dst) in enumerate(pairs)
    ]
    for copy in loads:
        copy.start()

    def remote(src, dst, send, recv, target):
        return pltpu.make_async_remote_copy(
            src_ref=src, dst_ref=dst, send_sem=send, recv_sem=recv,
            device_id=target, device_id_type=MESH,
        )

    def kv_copy(hop, a, b, src=None):
        by_last = a == 0 and hop == 0
        slot = hop + 2 * at_end if by_last else hop
        return remote(
            kv.at[0, a, part_rows(b)] if src is None else src, kv.at[slot, a, part_rows(b)],
            kv_send.at[hop, a, b], kv_recv.at[slot, a, b],
            (key_right if by_last else me + 1, grp),
        )

    def qo_copy(hop, a, b, src=None):
        slot = hop + 2 * at_start if a == 0 else hop
        return remote(
            qo.at[0, a, part_rows(b)] if src is None else src, qo.at[slot, a, part_rows(b)],
            qo_send.at[hop, a, b], qo_recv.at[slot, a, b],
            (query_left if a == 0 else me - 1, grp),
        )

    def arrived(buf, sems, slot, a, b):
        part, sem = buf.at[slot, a, part_rows(b)], sems.at[slot, a, b]
        remote(part, part, sem, sem, (me, core_mate)).wait_recv()

    not_first = jnp.logical_not(first_dev)
    not_last = jnp.logical_not(last_dev)
    inner = (me > 0) & (me < n_ctx - 1)

    def send_own_kv(b):
        @pl.when(not_last)
        def _():
            kv_copy(0, 0, b, k_hbm.at[part_rows(b)]).start()
            kv_copy(0, 1, b, v_hbm.at[part_rows(b)]).start()

    def send_own_qo(a, b):
        @pl.when(not_first)
        def _():
            qo_copy(0, a, b, (q_hbm if a == 0 else own_do).at[part_rows(b)]).start()

    def relay_kv(b):
        for a in range(2):
            @pl.when(not_first)
            def _():
                arrived(kv, kv_recv, 0, a, b)

            @pl.when(inner)
            def _():
                kv_copy(1, a, b).start()

    def wait_far_kv(b):
        for a in range(2):
            @pl.when(me > 1)
            def _():
                arrived(kv, kv_recv, 1, a, b)

    def forward_keys(hop, b):
        @pl.when(last_dev)
        def _():
            arrived(kv, kv_recv, hop + 2, 0, b)
            kv_copy(hop, 0, b, kv.at[hop + 2, 0, part_rows(b)]).start()

    def forward_queries(hop, b):
        @pl.when(first_dev)
        def _():
            arrived(qo, qo_recv, hop + 2, 0, b)
            qo_copy(hop, 0, b, qo.at[hop + 2, 0, part_rows(b)]).start()

    def relay_qo(a, b):
        arrived(qo, qo_recv, 0, a, b)

        @pl.when(me > 0)
        def _():
            qo_copy(1, a, b).start()

    def wait_far_qo(b):
        for a in range(2):
            @pl.when(me < n_ctx - 2)
            def _():
                arrived(qo, qo_recv, 1, a, b)

    def relay_do(b):
        @pl.when(not_last & jnp.logical_not(start_dev))
        def _():
            relay_qo(1, b)

    cot_core = remote(c_hbm, cot.at[1], cot_send.at[0], cot_recv.at[0], (me, core_mate))
    cot_x = remote(c_hbm, cot.at[2], cot_send.at[1], cot_recv.at[1], (me, x_mate))
    cot_relay = remote(cot.at[2], cot.at[3], cot_send.at[2], cot_recv.at[2], (me, core_mate))

    pl.semaphore_wait(barrier, greeted)

    @pl.when(end_dev)
    def _():
        for target in (half, half + 1, 0):
            greet((target, grp), seam_sem)

    @pl.when(before_end)
    def _():
        greet((half, grp), seam_sem)

    cot_x.start()
    cot_core.start()
    order = range(last, -1, -1)
    late_queries = end_dev | before_end
    for b in order:
        @pl.when(jnp.logical_not(end_dev))
        def _():
            send_own_qo(0, b)

        send_own_kv(b)

    @pl.when(first_dev)
    def _():
        kv[0] = jnp.zeros(kv.shape[1:], BF16)

    @pl.when(me <= 1)
    def _():
        kv[1] = jnp.zeros(kv.shape[1:], BF16)

    @pl.when(last_dev)
    def _():
        qo[0] = jnp.zeros(qo.shape[1:], BF16)
        stats_in[0] = jnp.zeros(stats_in.shape[1:], F32)

    @pl.when(me >= n_ctx - 2)
    def _():
        qo[1] = jnp.zeros(qo.shape[1:], BF16)
        stats_in[1] = jnp.zeros(stats_in.shape[1:], F32)

    base = me * rows
    q_pos = base + lax.broadcasted_iota(jnp.int32, (rows, 128), 0)
    first = jnp.zeros((rows, 128), jnp.int32)
    lists = offs[...]
    turned = pltpu.roll(lists, 128 - PREV, 1)
    lane = lax.broadcasted_iota(jnp.int32, lists.shape, 1)
    ahead = jnp.where(lane < 128 - PREV, turned, pltpu.roll(turned, lists.shape[0] - 1, 0))
    for g in range(groups):
        starts = jnp.broadcast_to(lists[g : g + 1, :], (rows, 128))
        later = jnp.broadcast_to(ahead[g : g + 1, :], (rows, 128))
        first = jnp.maximum(first, jnp.where(later <= q_pos, starts, 0))
    first = (first - base).astype(F32)
    low = jnp.max(first.T, axis=0, keepdims=True)
    stats[...] = jnp.zeros(stats.shape, F32)
    for b in order:
        stats[b, 2 * heads : 2 * heads + 1, :] = low[:, part_rows(b)]

    def w_block(index):
        return w_ref[:, pl.ds(pl.multiple_of(index * feats, feats), feats)]

    loads[0].wait()
    loads[1].wait()
    grad = dot_nt(cot[0], w_block(grp))
    cot_core.wait_recv()
    grad += dot_nt(cot[1], w_block(core_mate))

    @pl.when(not_last & jnp.logical_not(late_queries))
    def _():
        for b in order:
            relay_qo(0, b)

    @pl.when(jnp.logical_not(start_dev))
    def _():
        relay_kv(last)

    cot_x.wait_recv()
    cot_relay.start()
    grad += dot_nt(cot[2], w_block(x_mate))
    for b in order[:-1]:
        forward_keys(0, b)

    @pl.when(jnp.logical_not(start_dev))
    def _():
        for b in order[1:-1]:
            relay_kv(b)

    cot_relay.wait_recv()
    grad += dot_nt(cot[3], w_block(x_core_mate))
    own_do[...] = grad.astype(BF16)

    @pl.when(start_dev)
    def _():
        pl.semaphore_wait(seam_sem, 2)

    @pl.when(first_dev)
    def _():
        pl.semaphore_wait(seam_sem, 1)

    @pl.when(after_start)
    def _():
        pl.semaphore_wait(seam_sem, 1)

    @pl.when(end_dev)
    def _():
        relay_kv(0)

    for b in order:
        send_own_qo(1, b)

    @pl.when(end_dev)
    def _():
        for b in order:
            send_own_qo(0, b)

    @pl.when(start_dev)
    def _():
        for b in order:
            relay_kv(b)
            relay_qo(1, b)

    for b in order:
        forward_queries(0, b)
    for copy in loads[2:]:
        copy.wait()

    def head_cols(h):
        return slice(h * HD, (h + 1) * HD)

    def query_side(b):
        part = part_rows(b)
        floor = low[:, part]
        for h in range(heads):
            col = head_cols(h)
            query = own_q[part, col]
            grad_o = own_do[part, col]
            own_rows = slice(0, (b + 1) * BLOCK)
            far_rows = slice(b * BLOCK, rows)
            key_tiles = (own_k[own_rows, col], kv[0, 0, :, col], kv[1, 0, far_rows, col])
            value_tiles = (own_v[own_rows, col], kv[0, 1, :, col], kv[1, 1, far_rows, col])
            scores = []
            for d in range(3):
                shape = (key_tiles[d].shape[0], BLOCK)
                start = b * BLOCK if d == 2 else 0
                key_row = lax.broadcasted_iota(jnp.int32, shape, 0).astype(F32)
                mask = key_row >= floor + float(d * rows - start)
                if d == 0:
                    query_col = lax.broadcasted_iota(jnp.int32, shape, 1).astype(F32)
                    mask = mask & (key_row <= query_col + float(b * BLOCK))
                raw = dot_nt(key_tiles[d], query) * scale2
                scores.append(jnp.where(mask, raw, NEG_FILL))
            top = functools.reduce(
                jnp.maximum, [jnp.max(s, axis=0, keepdims=True) for s in scores]
            )
            expd = [jnp.exp2(s - top) for s in scores]
            total = functools.reduce(jnp.add, [jnp.sum(e, axis=0, keepdims=True) for e in expd])
            inverse = 1.0 / total
            probs = [e * inverse for e in expd]
            probs_b = [p.astype(BF16) for p in probs]
            mixed_t = sum(dot_tn(value_tiles[d], probs_b[d]) for d in range(3))
            attended = mixed_t.T.astype(BF16)
            att[part, col] = attended
            product = grad_o.astype(F32) * attended.astype(F32)
            delta = jnp.sum(product.T, axis=0, keepdims=True)
            stats[b, h : h + 1, :] = top + jnp.log2(total)
            stats[b, heads + h : heads + h + 1, :] = delta
            grads_b = []
            for d in range(3):
                grad_p = dot_nt(value_tiles[d], grad_o)
                grads_b.append((scale * probs[d] * (grad_p - delta)).astype(BF16))
            dq_t = sum(dot_tn(key_tiles[d], grads_b[d]) for d in range(3))
            out_ref[1, part, col] = dq_t.T.astype(BF16)
            grad_k = dot_nn(grads_b[0], query)
            grad_v = dot_nn(probs_b[0], grad_o)
            if b == last:
                acc[0, :, col] = grad_k
                acc[1, :, col] = grad_v
            else:
                acc[0, own_rows, col] += grad_k
                acc[1, own_rows, col] += grad_v

    def key_side(b):
        part = part_rows(b)
        for h in range(heads):
            col = head_cols(h)
            for d in range(2):
                start = b * BLOCK if d == 1 else 0
                near = slice(start, rows)
                query = qo[d, 0, part, col]
                grad_o = qo[d, 1, part, col]
                key_row = lax.broadcasted_iota(jnp.int32, (rows - start, BLOCK), 0).astype(F32)
                floor = stats_in[d, b, 2 * heads : 2 * heads + 1, :]
                floor = floor + float((d + 1) * rows - start)
                log_total = stats_in[d, b, h : h + 1, :]
                delta = stats_in[d, b, heads + h : heads + h + 1, :]
                raw = dot_nt(own_k[near, col], query) * scale2
                probs = jnp.where(key_row >= floor, jnp.exp2(raw - log_total), 0.0)
                acc[1, near, col] += dot_nn(probs.astype(BF16), grad_o)
                grad_p = dot_nt(own_v[near, col], grad_o)
                grad_s = (scale * probs * (grad_p - delta)).astype(BF16)
                acc[0, near, col] += dot_nn(grad_s, query)

    def stat_copy(b, d):
        return remote(
            stats.at[b], stats_in.at[d, b], st_send.at[d, b], st_recv.at[d, b], (me - 1 - d, grp)
        )

    def send_stats(b):
        for d in range(2):
            @pl.when(me > d)
            def _():
                stat_copy(b, d).start()

    def wait_queries(b):
        wait_far_qo(b)
        for d in range(2):
            @pl.when(me < n_ctx - 1 - d)
            def _():
                stat_copy(b, d).wait_recv()

    def mix_copy(i, b):
        part = part_rows(b)
        return remote(
            mix_out.at[i, part], mix_in.at[i, part], mix_send.at[i, b], mix_recv.at[i, b],
            (me, x_mate if i == 2 else core_mate),
        )

    def mix_near(b):
        part = part_rows(b)
        for i, owner in enumerate((x_core_mate, core_mate)):
            mix_out[i, part] = dot_nn(att[part], w_block(owner)).astype(BF16)
            mix_copy(i, b).start()

    def mix_far(b):
        part = part_rows(b)
        far_part = dot_nn(att[part], w_block(x_mate))
        mix_copy(0, b).wait_recv()
        mix_out[2, part] = (far_part + mix_in[0, part].astype(F32)).astype(BF16)
        mix_copy(2, b).start()

    def mix_finish(b):
        part = part_rows(b)
        own_part = dot_nn(att[part], w_block(grp))
        mix_copy(1, b).wait_recv()
        own_part += mix_in[1, part].astype(F32)
        mix_copy(2, b).wait_recv()
        out_ref[0, part] = (own_part + mix_in[2, part].astype(F32)).astype(BF16)

    for b in order:
        forward_queries(1, b)

    @pl.when(jnp.logical_not(end_dev | start_dev))
    def _():
        relay_kv(0)

    forward_keys(0, 0)
    relay_do(last)
    for b in order:
        wait_far_kv(b)
        query_side(b)
        send_stats(b)
        mix_near(b)
        if b == last:
            @pl.when(late_queries)
            def _():
                for late in order:
                    relay_qo(0, late)

            for later in order[1:]:
                relay_do(later)
        elif b > 0:
            wait_queries(b + 1)
            key_side(b + 1)
        mix_far(b)
    wait_queries(1)
    key_side(1)
    wait_queries(0)
    key_side(0)
    out_ref[2] = acc[0].astype(BF16)
    out_ref[3] = acc[1].astype(BF16)
    for b in order:
        mix_finish(b)

    cot_core.wait_send()
    cot_x.wait_send()
    cot_relay.wait_send()
    for b in order:
        kv_copy(0, 0, b).wait_send()
        qo_copy(0, 0, b).wait_send()

        @pl.when(not_last)
        def _():
            kv_copy(0, 1, b).wait_send()
            qo_copy(1, 0, b).wait_send()

        @pl.when(not_first)
        def _():
            qo_copy(0, 1, b).wait_send()

        @pl.when(inner)
        def _():
            kv_copy(1, 0, b).wait_send()
            kv_copy(1, 1, b).wait_send()
            qo_copy(1, 1, b).wait_send()

    for b in order:
        for d in range(2):
            @pl.when(me > d)
            def _():
                stat_copy(b, d).wait_send()
        for i in range(3):
            mix_copy(i, b).wait_send()


def spread(all_ref, *refs):
    outs, sems = refs[:-1], refs[-1]
    copies = [
        pltpu.make_async_copy(all_ref.at[i], out, sems.at[i]) for i, out in enumerate(outs)
    ]
    for copy in copies:
        copy.start()
    for copy in copies:
        copy.wait()


def per_device(n_ctx, queries, key_rows, value_rows, out_weight, cotangent, offsets):
    rows, feats = queries.shape
    blocks = rows // BLOCK
    count = offsets.shape[0]
    groups = -(-count // 128)
    padded = -(-(groups + 1) // 8) * 8
    offs = jnp.pad(offsets, (0, padded * 128 - count), constant_values=2**30)
    offs = offs.reshape(padded, 128)
    any_spec = pl.BlockSpec(memory_space=pl.ANY)
    vmem_spec = pl.BlockSpec(memory_space=pltpu.VMEM)
    tile = jax.ShapeDtypeStruct((rows, feats), BF16)
    dma = pltpu.SemaphoreType.DMA
    four = pl.pallas_call(
        functools.partial(kernel, n_ctx, groups),
        out_shape=jax.ShapeDtypeStruct((4, rows, feats), BF16),
        in_specs=[any_spec] * 5 + [vmem_spec],
        out_specs=vmem_spec,
        scratch_shapes=[
            pltpu.VMEM((rows, feats), BF16),
            pltpu.VMEM((rows, feats), BF16),
            pltpu.VMEM((rows, feats), BF16),
            pltpu.VMEM((rows, feats), BF16),
            pltpu.VMEM(out_weight.shape, BF16),
            pltpu.VMEM((4, rows, feats), BF16),
            pltpu.VMEM((4, 2, rows, feats), BF16),
            pltpu.VMEM((4, 2, rows, feats), BF16),
            pltpu.VMEM((blocks, 16, BLOCK), F32),
            pltpu.VMEM((2, blocks, 16, BLOCK), F32),
            pltpu.VMEM((rows, feats), BF16),
            pltpu.VMEM((2, rows, feats), F32),
            pltpu.VMEM((3, rows, feats), BF16),
            pltpu.VMEM((3, rows, feats), BF16),
            dma((5,)),
            dma((3,)),
            dma((3,)),
            dma((2, 2, blocks)),
            dma((4, 2, blocks)),
            dma((2, 2, blocks)),
            dma((4, 2, blocks)),
            dma((2, blocks)),
            dma((2, blocks)),
            dma((3, blocks)),
            dma((3, blocks)),
            pltpu.SemaphoreType.REGULAR,
        ],
        compiler_params=pltpu.CompilerParams(
            collective_id=0, has_side_effects=True, vmem_limit_bytes=58 * 1024 * 1024
        ),
    )(queries, key_rows, value_rows, out_weight, cotangent, offs)
    return pl.pallas_call(
        spread,
        out_shape=(tile,) * 4,
        in_specs=[vmem_spec],
        out_specs=(any_spec,) * 4,
        scratch_shapes=[dma((4,))],
    )(four)


def solution(mesh):
    in_specs = (
        P("ctx", "head"),
        P("ctx", "head"),
        P("ctx", "head"),
        P("head", None),
        P("ctx", "head"),
        P(),
    )
    out_specs = (P("ctx", "head"), P("ctx", "head"), P("ctx", "head"), P("ctx", "head"))
    return jax.shard_map(
        functools.partial(per_device, mesh.shape["ctx"]),
        mesh=mesh,
        in_specs=in_specs,
        out_specs=out_specs,
        check_vma=False,
    )
```
